32 devices in a mesh: scene: 2 (over x), gx: 16 (over z, y, core).
Axes of the slice: x: 2, y: 2, z: 4, core: 2. Of those that a mesh axis runs over, the one named last changes fastest.
Arguments:
- voxels: bfloat16 [64, 128, 8, 128], P(('scene', 'gx')), parts along dimension 0, may hold values from -6 to 6
- prior: float32 [64, 128, 8], P(('scene', 'gx')), parts along dimension 0, may hold values from -6 to 410
- conv_first: bfloat16 [27, 128, 128], replicated, may hold values from -0.109375 to 0.109375
- conv_second: bfloat16 [27, 128, 128], replicated, may hold values from -0.109375 to 0.109375
- score_x: bfloat16 [128, 128], replicated, may hold values from -2 to 2
- score_y: bfloat16 [128, 128], replicated, may hold values from -1.5 to 1.5
- plane_yz_w: bfloat16 [9, 128, 128], replicated, may hold values from -0.1875 to 0.1875
- plane_xz_w: bfloat16 [9, 128, 128], replicated, may hold values from -0.1875 to 0.1875
- norm_gain: float32 [128], replicated, may hold values from 0.1 to 1.9
- mlp_in: bfloat16 [128, 512], replicated, may hold values from -0.5 to 0.5
- mlp_out: bfloat16 [512, 128], replicated, may hold values from -0.25 to 0.25
Outputs:
- encoded: bfloat16 [64, 128, 8, 128], P(('scene', 'gx')), parts along dimension 0
The draws below stay inside these ranges and needn't reach their ends.
There are 2 independent parts, one for each index of `scene`. The reference program is written for one: setup_inputs(seed, part) draws one part's arguments, and reference() takes and returns one part's arrays. A program takes and returns all parts, laid end to end along the dimension named above; an argument that names none is the same for every part. Nothing has to cross between parts.
All inputs are finite; a program needn't handle non-finite values.
Results may differ from the reference program's by a relative error of at most 0.012.
Values may be sent and summed in bfloat16 or wider, within the bound.
A program may use at most 64 MiB of HBM per device.

```python
import jax
import jax.numpy as jnp
from jax import lax

C = 128
FF = 512
Y = 128
Z = 8
X = 32


def draw_prior(key, part):
    field_key = jax.random.fold_in(key, 11)
    field = jnp.clip(jax.random.normal(field_key, (X, Y, Z), jnp.float32) * 1.5, -6.0, 6.0)
    return field


def draw_voxels(key, part):
    field_key = jax.random.fold_in(key, 31)
    field = jnp.clip(jax.random.normal(field_key, (X, Y, Z, C), jnp.float32), -6.0, 6.0)
    return field.astype(jnp.bfloat16)


def draw_score_x(key, part):
    spread = float(C // 9) ** (-0.5)
    base = jax.random.normal(jax.random.fold_in(key, 41), (C, C), jnp.float32) * spread
    base = jnp.clip(base, -6.0 * spread, 6.0 * spread)
    return base.astype(jnp.bfloat16)


def bell_draw(own_key, dims, scale, most, kind=jnp.bfloat16):
    drawn = scale * jax.random.normal(own_key, dims, jnp.float32)
    return jnp.clip(drawn, min=-most, max=most).astype(kind)


def setup_inputs(seed: int = 0, part: int = 0) -> dict:
    key_of = jax.random.split(jax.random.key(seed), 12)
    part_splits = jax.random.split(jax.random.fold_in(key_of[11], part), 12)
    return {
        "voxels": draw_voxels(jax.random.fold_in(jax.random.fold_in(key_of[11], part), 71), part),
        "prior": draw_prior(jax.random.fold_in(jax.random.fold_in(key_of[11], part), 71), part),
        "conv_first": bell_draw(key_of[2], (27, C, C), (27 * C) ** -0.5, 0.109375),
        "conv_second": bell_draw(key_of[3], (27, C, C), (27 * C) ** -0.5, 0.109375),
        "score_x": draw_score_x(jax.random.fold_in(key_of[11], 71), part),
        "score_y": bell_draw(key_of[5], (C, C), (C // 9) ** -0.5, 1.5),
        "plane_yz_w": bell_draw(key_of[6], (9, C, C), (9 * C) ** -0.5, 0.1875),
        "plane_xz_w": bell_draw(key_of[7], (9, C, C), (9 * C) ** -0.5, 0.1875),
        "norm_gain": jnp.clip(1.0 + 0.18 * jax.random.normal(key_of[8], (C,), jnp.float32), 0.1, 1.9),
        "mlp_in": bell_draw(key_of[9], (C, FF), C ** -0.5, 0.5),
        "mlp_out": bell_draw(key_of[10], (FF, C), FF ** -0.5, 0.25),
    }


def activate(values):
    return jax.nn.gelu(values, approximate=True)

def volume(field, weight):
    channels = weight.shape[-1]
    kernel = weight.astype(jnp.float32).reshape(3, 3, 3, channels, channels)
    result = lax.conv_general_dilated(field.astype(jnp.float32)[None], kernel, (1, 1, 1), [(1, 1), (1, 1), (1, 1)], dimension_numbers=('NDHWC', 'DHWIO', 'NDHWC'), precision=lax.Precision.HIGHEST)
    return result[0]

def planar(field, weight):
    channels = weight.shape[-1]
    kernel = weight.astype(jnp.float32).reshape(3, 3, channels, channels)
    result = lax.conv_general_dilated(field.astype(jnp.float32)[None], kernel, (1, 1), [(1, 1), (1, 1)], dimension_numbers=('NHWC', 'HWIO', 'NHWC'), precision=lax.Precision.HIGHEST)
    return result[0]

def reference(voxels, prior, conv_first, conv_second, score_x, score_y, plane_yz_w, plane_xz_w, norm_gain, mlp_in, mlp_out):
    first = activate(volume(voxels, conv_first)).astype(jnp.bfloat16)
    feature = (volume(first, conv_second) + voxels.astype(jnp.float32)).astype(jnp.bfloat16)
    flat = feature.reshape(-1, C)
    logit_x = jnp.dot(flat, score_x, preferred_element_type=jnp.float32).reshape(feature.shape) + prior[..., None]
    logit_y = jnp.dot(flat, score_y, preferred_element_type=jnp.float32).reshape(feature.shape) + prior[..., None]
    feature_f = feature.astype(jnp.float32)
    pooled_yz = lax.optimization_barrier(jnp.sum(jax.nn.softmax(logit_x, axis=0) * feature_f, axis=0)).astype(jnp.bfloat16)
    pooled_xz = lax.optimization_barrier(jnp.sum(jax.nn.softmax(logit_y, axis=1) * feature_f, axis=1)).astype(jnp.bfloat16)
    plane_yz = planar(pooled_yz, plane_yz_w).astype(jnp.bfloat16)
    plane_xz = planar(pooled_xz, plane_xz_w).astype(jnp.bfloat16)
    joined = feature_f * (plane_yz.astype(jnp.float32)[None] + plane_xz.astype(jnp.float32)[:, None])
    scale = lax.rsqrt(lax.optimization_barrier(jnp.mean(joined * joined, axis=-1, keepdims=True)) + 1e-06)
    normed = (joined * scale * norm_gain).astype(jnp.bfloat16)
    hidden = activate(jnp.dot(normed.reshape(-1, C), mlp_in, preferred_element_type=jnp.float32)).astype(jnp.bfloat16)
    update = jnp.dot(hidden, mlp_out, preferred_element_type=jnp.float32).reshape(joined.shape)
    return (joined + update).astype(jnp.bfloat16)
```

```python
import functools

import jax
import jax.numpy as jnp
from jax import lax
from jax.experimental import pallas as pl
from jax.experimental.pallas import tpu as pltpu
from jax.sharding import PartitionSpec as P

MESH = pl.DeviceIdType.MESH
PAD = 16
F32 = jnp.float32
BF16 = jnp.bfloat16


def activate(values):
    return jax.nn.gelu(values, approximate=True)


def stages_of(length, devices):
    stages, distance = [], 1
    while distance < devices:
        halves = length // 2 >= 16 and (length // 2) % 16 == 0
        length = length // 2 if halves else length
        stages.append((distance, length, halves))
        distance *= 2
    return stages


def shifted(values, depth):
    rows = values.shape[0]
    at_z = lax.broadcasted_iota(jnp.int32, values.shape, 0) % depth
    below = jnp.where(at_z == 0, 0.0, pltpu.roll(values, 1, 0))
    above = jnp.where(at_z == depth - 1, 0.0, pltpu.roll(values, rows - 1, 0))
    return below, values, above


def neighbourhood(padded, start, tile, depth):
    window = padded[pl.ds(pl.multiple_of(start, 16), tile + 2 * PAD), :].astype(F32)
    parts = shifted(window, depth)
    columns = []
    for along in (-1, 0, 1):
        first = PAD + along * depth
        for part in parts:
            columns.append(part[first : first + tile].astype(BF16))
    return jnp.concatenate(columns, axis=1)


def dot(a, b):
    return jnp.dot(a, b, preferred_element_type=F32)


def kernel(
    n,
    tile,
    stages,
    voxels,
    prior,
    conv_first,
    conv_second,
    score_x,
    score_y,
    plane_yz_w,
    plane_xz_w,
    norm_gain,
    mlp_in,
    mlp_out,
    out,
    w_first,
    w_second,
    w_score,
    w_yz,
    w_xz,
    w_in,
    w_out,
    vox,
    face_vox,
    first,
    face_first,
    acc,
    feature,
    stats,
    pooled,
    strip,
    halves,
    load_sem,
    vox_sem,
    face_send,
    face_recv,
    strip_send,
    strip_recv,
    rs_send,
    rs_recv,
    ag_send,
    ag_recv,
):
    me = lax.axis_index("gx")
    length, channels = voxels.shape[1], voxels.shape[2]
    depth = prior.shape[2]
    tiles = length // tile
    has_left, has_right = me > 0, me < n - 1
    left, right = me - 1, me + 1
    bits = [(me // distance) % 2 for distance, _, _ in stages]
    partners = [me + (1 - 2 * bit) * stage[0] for bit, stage in zip(bits, stages)]

    loads = [
        (conv_first.at[tap], w_first.at[:, pl.ds((2 - tap) * channels, channels)]) for tap in range(3)
    ]
    loads += [
        (conv_second.at[tap], w_second.at[:, pl.ds((2 - tap) * channels, channels)])
        for tap in range(3)
    ]
    loads += [
        (score_x, w_score.at[:, pl.ds(0, channels)]),
        (score_y, w_score.at[:, pl.ds(channels, channels)]),
        (plane_yz_w, w_yz),
        (plane_xz_w, w_xz),
        (mlp_in, w_in),
        (mlp_out, w_out),
    ]
    vox_loads = [
        pltpu.make_async_copy(
            voxels.at[row], vox.at[row, pl.ds(PAD, length), :], vox_sem.at[row]
        )
        for row in range(2)
    ]
    loads = [
        pltpu.make_async_copy(source, target, load_sem.at[i])
        for i, (source, target) in enumerate(loads)
    ]
    for copy in vox_loads + loads:
        copy.start()

    barrier = pltpu.get_barrier_semaphore()
    for partner in partners:
        pl.semaphore_signal(barrier, inc=1, device_id={"gx": partner}, device_id_type=MESH)

    @pl.when(has_left)
    def _():
        pl.semaphore_signal(barrier, inc=1, device_id={"gx": left}, device_id_type=MESH)

    @pl.when(has_right)
    def _():
        pl.semaphore_signal(barrier, inc=1, device_id={"gx": right}, device_id_type=MESH)

    edge = jnp.zeros((2, PAD, channels), BF16)
    for padded in (vox, face_vox, first, face_first):
        padded[:, 0:PAD, :] = edge
        padded[:, PAD + length :, :] = edge
    pooled[0:PAD, :] = edge[0]
    pooled[PAD + length :, :] = edge[0]

    for side, has in ((0, has_left), (1, has_right)):

        @pl.when(jnp.logical_not(has))
        def _():
            blank = jnp.zeros((length, channels), BF16)
            face_vox[side, pl.ds(PAD, length), :] = blank
            face_first[side, pl.ds(PAD, length), :] = blank
            strip[3 * side] = jnp.zeros(strip.shape[1:], F32)

    pl.semaphore_wait(barrier, len(stages) + jnp.where(has_left, 1, 0) + jnp.where(has_right, 1, 0))

    def face_copy(which, source, target, side, t, to):
        return pltpu.make_async_remote_copy(
            src_ref=source,
            dst_ref=target.at[1 - side, pl.ds(pl.multiple_of(PAD + t * tile, 16), tile), :],
            send_sem=face_send.at[which, side, t],
            recv_sem=face_recv.at[which, 1 - side, t],
            device_id={"gx": to},
            device_id_type=MESH,
        )

    def vox_copy(side, t):
        source = voxels.at[side, pl.ds(pl.multiple_of(t * tile, 16), tile), :]
        return face_copy(0, source, face_vox, side, t, (left, right)[side])

    def first_copy(side, t):
        source = first.at[side, pl.ds(pl.multiple_of(PAD + t * tile, 16), tile), :]
        return face_copy(1, source, face_first, side, t, (left, right)[side])

    def arrive(make, side, t, has):
        @pl.when(has)
        def _():
            make(1 - side, t).wait_recv()

    def sent(make):
        for side, has in ((0, has_left), (1, has_right)):

            @pl.when(has)
            def _():
                for t in range(tiles):
                    make(side, t).wait_send()

    for t in range(tiles):
        for side, has in ((0, has_left), (1, has_right)):

            @pl.when(has)
            def _():
                vox_copy(side, t).start()

    def inner(source, weight):
        def body(t, _):
            start = t * tile
            total = dot(neighbourhood(source.at[0], start, tile, depth), weight[:, channels:])
            total += dot(
                neighbourhood(source.at[1], start, tile, depth), weight[:, : 2 * channels]
            )
            acc[pl.ds(pl.multiple_of(start, 16), tile), :] = total
            return 0

        lax.fori_loop(0, tiles, body, 0)

    def outer(face, make, weight, side, t):
        has = (has_left, has_right)[side]
        if isinstance(t, int) and t == 0:
            arrive(make, side, 0, has)
        if t + 1 < tiles:
            arrive(make, side, t + 1, has)
        start = t * tile
        low = 2 * channels * (1 - side)
        return acc[start : start + tile, side * channels : (side + 1) * channels] + dot(
            neighbourhood(face.at[side], start, tile, depth), weight[:, low : low + channels]
        )

    for copy in vox_loads + loads[:3]:
        copy.wait()
    inner(vox, w_first)
    for t in range(tiles):
        for side, has in ((0, has_left), (1, has_right)):
            value = activate(outer(face_vox, vox_copy, w_first, side, t)).astype(BF16)
            first[side, PAD + t * tile : PAD + (t + 1) * tile, :] = value

            @pl.when(has)
            def _():
                first_copy(side, t).start()

    for copy in loads[3:]:
        copy.wait()
    inner(first, w_second)

    cells = tile // depth
    eye = lax.broadcasted_iota(jnp.int32, (cells, depth, depth), 1) == lax.broadcasted_iota(
        jnp.int32, (cells, depth, depth), 2
    )
    running = [None, None]
    for t in range(tiles):
        logits, features = [], []
        for side in range(2):
            start = PAD + t * tile
            value = outer(face_first, first_copy, w_second, side, t)
            value += vox[side, start : start + tile, :].astype(F32)
            value = value.astype(BF16)
            feature[side, t * tile : (t + 1) * tile, :] = value
            both = dot(value, w_score[...])
            field = prior[side, t * cells : (t + 1) * cells, :]
            field = jnp.broadcast_to(field[:, None, :], (cells, depth, depth))
            field = jnp.sum(jnp.where(eye, field, 0.0), axis=2, keepdims=True)
            field = jnp.broadcast_to(field, (cells, depth, channels))
            value = value.astype(F32)
            logits.append(both[:, :channels] + field.reshape(tile, channels))
            features.append(value)
            logit_y = both[:, channels:].reshape(cells, depth, channels) + field
            value = value.reshape(cells, depth, channels)
            peak = jnp.max(logit_y, axis=0)
            if running[side] is None:
                weight = jnp.exp(logit_y - peak[None])
                running[side] = (peak, jnp.sum(weight, 0), jnp.sum(weight * value, 0))
            else:
                old, norm, total = running[side]
                peak = jnp.maximum(peak, old)
                weight = jnp.exp(logit_y - peak[None])
                keep = jnp.exp(old - peak)
                running[side] = (
                    peak,
                    norm * keep + jnp.sum(weight, 0),
                    total * keep + jnp.sum(weight * value, 0),
                )
        peak = jnp.maximum(logits[0], logits[1]).astype(BF16)
        weights = [jnp.exp(logit - peak.astype(F32)) for logit in logits]
        at = slice(t * tile, (t + 1) * tile)
        stats[0, at, :] = peak
        stats[1, at, :] = (weights[0] + weights[1]).astype(BF16)
        stats[2, at, :] = (weights[0] * features[0] + weights[1] * features[1]).astype(BF16)

    def reduce_copy(k, start):
        rows = stages[k][1]
        return pltpu.make_async_remote_copy(
            src_ref=stats.at[:, pl.ds(pl.multiple_of(start, 16), rows), :],
            dst_ref=halves[k],
            send_sem=rs_send.at[k],
            recv_sem=rs_recv.at[k],
            device_id={"gx": partners[k]},
            device_id_type=MESH,
        )

    for side in range(2):
        _, norm, total = running[side]
        strip[1 + side] = (total / norm).astype(BF16).astype(F32)

    def strip_copy(side):
        return pltpu.make_async_remote_copy(
            src_ref=strip.at[1 + side],
            dst_ref=strip.at[3 - 3 * side],
            send_sem=strip_send.at[side],
            recv_sem=strip_recv.at[1 - side],
            device_id={"gx": (left, right)[side]},
            device_id_type=MESH,
        )

    start = 0
    pending = []
    for k, (distance, rows, halved) in enumerate(stages):
        if halved:
            give, keep = start + (1 - bits[k]) * rows, start + bits[k] * rows
        else:
            give = keep = start
        copy = reduce_copy(k, give)
        copy.start()
        pending.append(copy)
        if k == 0:
            for side, has in ((0, has_left), (1, has_right)):

                @pl.when(has)
                def _():
                    strip_copy(side).start()

        copy.wait_recv()
        if not halved:
            copy.wait_send()
            pending.pop()
        start = pl.multiple_of(keep, 16)
        mine = stats[:, pl.ds(start, rows), :].astype(F32)
        other = halves[k][...].astype(F32)
        peak = jnp.maximum(mine[0], other[0])
        up, down = jnp.exp(mine[0] - peak), jnp.exp(other[0] - peak)
        norm = mine[1] * up + other[1] * down
        total = mine[2] * up + other[2] * down
        if k + 1 < len(stages):
            stats[:, pl.ds(start, rows), :] = jnp.stack([peak, norm, total]).astype(BF16)
        else:
            pooled[pl.ds(pl.multiple_of(PAD + start, 16), rows), :] = (total / norm).astype(BF16)

    for k, (distance, rows, halved) in reversed(list(enumerate(stages))):
        if not halved:
            continue
        part = pooled.at[pl.ds(pl.multiple_of(PAD + start, 16), rows), :]
        copy = pltpu.make_async_remote_copy(
            src_ref=part,
            dst_ref=part,
            send_sem=ag_send.at[k],
            recv_sem=ag_recv.at[k],
            device_id={"gx": partners[k]},
            device_id_type=MESH,
        )
        copy.start()
        pending.append(copy)
        copy.wait_recv()
        start = start - bits[k] * rows

    for side, has in ((0, has_left), (1, has_right)):

        @pl.when(has)
        def _():
            strip_copy(1 - side).wait_recv()

    rows_z = [shifted(strip[i], depth) for i in range(4)]
    stacked = [
        jnp.concatenate([part for i in range(3) for part in rows_z[x + i]], axis=1)
        for x in range(2)
    ]
    plane_xz = dot(jnp.concatenate(stacked, axis=0).astype(BF16), w_xz[...])
    plane_xz = plane_xz.astype(BF16).astype(F32)
    gain = norm_gain[...]

    def finish(t, _):
        at = pl.ds(pl.multiple_of(t * tile, 16), tile)
        plane_yz = dot(neighbourhood(pooled, t * tile, tile, depth), w_yz[...])
        plane_yz = plane_yz.astype(BF16).astype(F32).reshape(cells, depth, channels)
        for side in range(2):
            mixing = plane_yz + plane_xz[side * depth : (side + 1) * depth][None]
            joined = feature[side, at, :].astype(F32) * mixing.reshape(tile, channels)
            scale = lax.rsqrt(jnp.mean(joined * joined, axis=-1, keepdims=True) + 1e-06)
            normed = (joined * scale * gain).astype(BF16)
            hidden = activate(dot(normed, w_in[...])).astype(BF16)
            out[side, at, :] = (joined + dot(hidden, w_out[...])).astype(BF16)
        return 0

    lax.fori_loop(0, tiles, finish, 0)

    for copy in pending:
        copy.wait_send()
    sent(vox_copy)
    sent(first_copy)
    for side, has in ((0, has_left), (1, has_right)):

        @pl.when(has)
        def _():
            strip_copy(side).wait_send()


def on_device(
    n,
    voxels,
    prior,
    conv_first,
    conv_second,
    score_x,
    score_y,
    plane_yz_w,
    plane_xz_w,
    norm_gain,
    mlp_in,
    mlp_out,
):
    rows, across, depth, channels = voxels.shape
    assert rows == 2 and depth == 8 and n & (n - 1) == 0
    length = across * depth
    hidden = mlp_in.shape[1]
    tile = min(256, length)
    tiles = length // tile
    stages = stages_of(length, n)
    padded = length + 2 * PAD
    taps = conv_first.shape[0] // 3 * channels
    hbm = pl.BlockSpec(memory_space=pl.ANY)
    vmem = pl.BlockSpec(memory_space=pltpu.VMEM)
    result = pl.pallas_call(
        functools.partial(kernel, n, tile, stages),
        out_shape=jax.ShapeDtypeStruct((rows, length, channels), BF16),
        in_specs=[hbm, vmem, hbm, hbm, hbm, hbm, hbm, hbm, vmem, hbm, hbm],
        out_specs=vmem,
        scratch_shapes=[
            pltpu.VMEM((taps, 3 * channels), BF16),
            pltpu.VMEM((taps, 3 * channels), BF16),
            pltpu.VMEM((channels, 2 * channels), BF16),
            pltpu.VMEM((taps, channels), BF16),
            pltpu.VMEM((taps, channels), BF16),
            pltpu.VMEM((channels, hidden), BF16),
            pltpu.VMEM((hidden, channels), BF16),
            pltpu.VMEM((2, padded, channels), BF16),
            pltpu.VMEM((2, padded, channels), BF16),
            pltpu.VMEM((2, padded, channels), BF16),
            pltpu.VMEM((2, padded, channels), BF16),
            pltpu.VMEM((length, 2 * channels), F32),
            pltpu.VMEM((2, length, channels), BF16),
            pltpu.VMEM((3, length, channels), BF16),
            pltpu.VMEM((padded, channels), BF16),
            pltpu.VMEM((4, depth, channels), F32),
            [pltpu.VMEM((3, stage[1], channels), BF16) for stage in stages],
            pltpu.SemaphoreType.DMA((12,)),
            pltpu.SemaphoreType.DMA((2,)),
            pltpu.SemaphoreType.DMA((2, 2, tiles)),
            pltpu.SemaphoreType.DMA((2, 2, tiles)),
            pltpu.SemaphoreType.DMA((2,)),
            pltpu.SemaphoreType.DMA((2,)),
            pltpu.SemaphoreType.DMA((len(stages),)),
            pltpu.SemaphoreType.DMA((len(stages),)),
            pltpu.SemaphoreType.DMA((len(stages),)),
            pltpu.SemaphoreType.DMA((len(stages),)),
        ],
        compiler_params=pltpu.CompilerParams(
            collective_id=0, has_side_effects=True, vmem_limit_bytes=48 * 1024 * 1024
        ),
    )(
        voxels.reshape(rows, length, channels),
        prior,
        conv_first.reshape(3, taps, channels),
        conv_second.reshape(3, taps, channels),
        score_x,
        score_y,
        plane_yz_w.reshape(taps, channels),
        plane_xz_w.reshape(taps, channels),
        norm_gain.reshape(1, channels),
        mlp_in,
        mlp_out,
    )
    return result.reshape(voxels.shape)


def solution(mesh):
    split = P(("scene", "gx"), None, None, None)
    return jax.shard_map(
        functools.partial(on_device, mesh.shape["gx"]),
        mesh=mesh,
        in_specs=(split, P(("scene", "gx"), None, None)) + (P(),) * 9,
        out_specs=split,
        check_vma=False,
    )
```

```python
import functools

import jax
import jax.numpy as jnp
from jax import lax
from jax.experimental import pallas as pl
from jax.experimental.pallas import tpu as pltpu
from jax.sharding import PartitionSpec as P

MESH = pl.DeviceIdType.MESH
PAD = 16
F32 = jnp.float32
BF16 = jnp.bfloat16


def activate(values):
    return jax.nn.gelu(values, approximate=True)


def stages_of(rows, devices):
    count = devices.bit_length() - 1
    bits = [[i] for i in range(min(2, count))]
    bits += [list(range(i, min(i + 2, count))) for i in range(2, count, 2)]
    stages = []
    for group in bits:
        radix = 1 << len(group)
        shares = rows % (16 * radix) == 0
        rows = rows // radix if shares else rows
        stages.append((1 << group[0], radix, rows, shares))
    return stages


def far_radix(stages):
    total = 1
    for distance, radix, _, shares in stages:
        if shares and distance > 1:
            total *= radix
    return total


def shifted(values, depth):
    rows = values.shape[0]
    at_z = lax.broadcasted_iota(jnp.int32, values.shape, 0) % depth
    below = jnp.where(at_z == 0, 0.0, pltpu.roll(values, 1, 0))
    above = jnp.where(at_z == depth - 1, 0.0, pltpu.roll(values, rows - 1, 0))
    return below, values, above


def neighbourhood(padded, start, tile, depth):
    window = padded[pl.ds(pl.multiple_of(start, 16), tile + 2 * PAD), :].astype(F32)
    parts = shifted(window, depth)
    columns = []
    for along in (-1, 0, 1):
        first = PAD + along * depth
        for part in parts:
            columns.append(part[first : first + tile].astype(BF16))
    return jnp.concatenate(columns, axis=1)


def dot(a, b):
    return jnp.dot(a, b, preferred_element_type=F32)


def kernel(
    n,
    tile,
    stages,
    voxels,
    prior,
    conv_first,
    conv_second,
    score_x,
    score_y,
    plane_yz_w,
    plane_xz_w,
    norm_gain,
    mlp_in,
    mlp_out,
    out,
    w_first,
    w_second,
    w_score,
    w_yz,
    w_xz,
    w_in,
    w_out,
    vox,
    face_vox,
    first,
    face_first,
    acc,
    feature,
    stats,
    pooled,
    strip,
    halves,
    load_sem,
    vox_sem,
    face_send,
    face_recv,
    strip_send,
    strip_recv,
    rs_send,
    rs_recv,
    ag_send,
    ag_recv,
):
    me = lax.axis_index("gx")
    length, channels = voxels.shape[1], voxels.shape[2]
    depth = prior.shape[1]
    tiles = length // tile
    has_left, has_right = me > 0, me < n - 1
    left, right = me - 1, me + 1
    across = length // depth

    def across_bits(distance, hop):
        other, weight = me, 1
        while weight <= hop:
            bit = (me // (distance * weight)) % 2
            if hop & weight:
                other = other + (1 - 2 * bit) * distance * weight
            weight *= 2
        return other

    digits = [(me // distance) % radix for distance, radix, _, _ in stages]
    partners = []
    for distance, radix, _, _ in stages:
        found = {}
        for hop in range(1, radix):
            other = across_bits(distance, hop)
            found[hop] = (other, (other // distance) % radix)
        partners.append(found)
    slots = [sum(stage[1] - 1 for stage in stages[:k]) for k in range(len(stages))]
    far = [across_bits(2, hop) for hop in range(1, far_radix(stages))]

    loads = [
        (conv_first.at[tap], w_first.at[:, pl.ds((2 - tap) * channels, channels)]) for tap in range(3)
    ]
    loads += [
        (conv_second.at[tap], w_second.at[:, pl.ds((2 - tap) * channels, channels)])
        for tap in range(3)
    ]
    loads += [
        (score_x, w_score.at[:, pl.ds(0, channels)]),
        (score_y, w_score.at[:, pl.ds(channels, channels)]),
        (plane_yz_w, w_yz),
        (plane_xz_w, w_xz),
        (mlp_in, w_in),
        (mlp_out, w_out),
    ]
    vox_loads = [
        pltpu.make_async_copy(
            voxels.at[row], vox.at[row, pl.ds(PAD, length), :], vox_sem.at[row]
        )
        for row in range(2)
    ]
    loads = [
        pltpu.make_async_copy(source, target, load_sem.at[i])
        for i, (source, target) in enumerate(loads)
    ]
    for copy in vox_loads + loads:
        copy.start()

    barrier = pltpu.get_barrier_semaphore()
    greeted = far + [
        partner
        for stage, found in zip(stages, partners)
        for partner, _ in found.values()
        if stage[0] == 1 or not stage[3]
    ]
    for partner in greeted:
        pl.semaphore_signal(barrier, inc=1, device_id={"gx": partner}, device_id_type=MESH)

    @pl.when(has_left)
    def _():
        pl.semaphore_signal(barrier, inc=1, device_id={"gx": left}, device_id_type=MESH)

    @pl.when(has_right)
    def _():
        pl.semaphore_signal(barrier, inc=1, device_id={"gx": right}, device_id_type=MESH)

    edge = jnp.zeros((2, PAD, channels), BF16)
    for padded in (vox, face_vox, first, face_first):
        padded[:, 0:PAD, :] = edge
        padded[:, PAD + length :, :] = edge
    pooled[0:PAD, :] = edge[0]
    pooled[PAD + length :, :] = edge[0]

    for side, has in ((0, has_left), (1, has_right)):

        @pl.when(jnp.logical_not(has))
        def _():
            blank = jnp.zeros((length, channels), BF16)
            face_vox[side, pl.ds(PAD, length), :] = blank
            face_first[side, pl.ds(PAD, length), :] = blank
            strip[3 * side] = jnp.zeros(strip.shape[1:], F32)

    pl.semaphore_wait(barrier, len(greeted) + jnp.where(has_left, 1, 0) + jnp.where(has_right, 1, 0))

    def face_copy(which, source, target, side, t, to):
        return pltpu.make_async_remote_copy(
            src_ref=source,
            dst_ref=target.at[1 - side, pl.ds(pl.multiple_of(PAD + t * tile, 16), tile), :],
            send_sem=face_send.at[which, side, t],
            recv_sem=face_recv.at[which, 1 - side, t],
            device_id={"gx": to},
            device_id_type=MESH,
        )

    def vox_copy(side, t):
        source = voxels.at[side, pl.ds(pl.multiple_of(t * tile, 16), tile), :]
        return face_copy(0, source, face_vox, side, t, (left, right)[side])

    def first_copy(side, t):
        source = first.at[side, pl.ds(pl.multiple_of(PAD + t * tile, 16), tile), :]
        return face_copy(1, source, face_first, side, t, (left, right)[side])

    def arrive(make, side, t, has):
        @pl.when(has)
        def _():
            make(1 - side, t).wait_recv()

    def sent(make):
        for side, has in ((0, has_left), (1, has_right)):

            @pl.when(has)
            def _():
                for t in range(tiles):
                    make(side, t).wait_send()

    for t in range(tiles):
        for side, has in ((0, has_left), (1, has_right)):

            @pl.when(has)
            def _():
                vox_copy(side, t).start()

    def inner(source, weight):
        def body(t, _):
            start = t * tile
            total = dot(neighbourhood(source.at[0], start, tile, depth), weight[:, channels:])
            total += dot(
                neighbourhood(source.at[1], start, tile, depth), weight[:, : 2 * channels]
            )
            acc[pl.ds(pl.multiple_of(start, 16), tile), :] = total
            return 0

        lax.fori_loop(0, tiles, body, 0)

    def outer(face, make, weight, side, t):
        has = (has_left, has_right)[side]
        if isinstance(t, int) and t == 0:
            arrive(make, side, 0, has)
        if t + 1 < tiles:
            arrive(make, side, t + 1, has)
        start = t * tile
        low = 2 * channels * (1 - side)
        return acc[start : start + tile, side * channels : (side + 1) * channels] + dot(
            neighbourhood(face.at[side], start, tile, depth), weight[:, low : low + channels]
        )

    for copy in vox_loads + loads[:3]:
        copy.wait()
    inner(vox, w_first)
    for t in range(tiles):
        for side, has in ((0, has_left), (1, has_right)):
            value = activate(outer(face_vox, vox_copy, w_first, side, t)).astype(BF16)
            first[side, PAD + t * tile : PAD + (t + 1) * tile, :] = value

            @pl.when(has)
            def _():
                first_copy(side, t).start()

    for copy in loads[3:]:
        copy.wait()
    inner(first, w_second)

    cells = tile // depth
    cube = (cells, depth, across)
    lane = lax.broadcasted_iota(jnp.int32, cube, 2)
    cell = lax.broadcasted_iota(jnp.int32, cube, 0)
    running = [None, None]

    def local_part(t):
        logits, features = [], []
        for side in range(2):
            start = PAD + t * tile
            value = outer(face_first, first_copy, w_second, side, t)
            value += vox[side, start : start + tile, :].astype(F32)
            value = value.astype(BF16)
            feature[side, t * tile : (t + 1) * tile, :] = value
            both = dot(value, w_score[...])
            field = jnp.broadcast_to(prior[side][None], cube)
            field = jnp.where(lane == cell + t * cells, field, 0.0)
            field = jnp.sum(field, axis=2, keepdims=True)
            field = jnp.broadcast_to(field, (cells, depth, channels))
            value = value.astype(F32)
            logits.append(both[:, :channels] + field.reshape(tile, channels))
            features.append(value)
            logit_y = both[:, channels:].reshape(cells, depth, channels) + field
            value = value.reshape(cells, depth, channels)
            peak = jnp.max(logit_y, axis=0)
            if running[side] is None:
                weight = jnp.exp(logit_y - peak[None])
                running[side] = (peak, jnp.sum(weight, 0), jnp.sum(weight * value, 0))
            else:
                old, norm, total = running[side]
                peak = jnp.maximum(peak, old)
                weight = jnp.exp(logit_y - peak[None])
                keep = jnp.exp(old - peak)
                running[side] = (
                    peak,
                    norm * keep + jnp.sum(weight, 0),
                    total * keep + jnp.sum(weight * value, 0),
                )
        peak = jnp.maximum(logits[0], logits[1]).astype(BF16)
        weights = [jnp.exp(logit - peak.astype(F32)) for logit in logits]
        at = slice(t * tile, (t + 1) * tile)
        stats[0, at, :] = peak
        stats[1, at, :] = (weights[0] + weights[1]).astype(BF16)
        stats[2, at, :] = (weights[0] * features[0] + weights[1] * features[1]).astype(BF16)

    def rows_at(start, rows):
        return pl.ds(pl.multiple_of(start, 16), rows)

    starts = [t * tile for t in range(tiles)]
    pending = []
    flying = {}

    def reduce_start(g, k):
        distance, radix, rows, shares = stages[k]
        mine = digits[k]
        copies = []
        for hop in range(1, radix):
            partner, theirs = partners[k][hop]
            give = starts[g] + theirs * rows if shares else starts[g]
            copy = pltpu.make_async_remote_copy(
                src_ref=stats.at[:, rows_at(give, rows), :],
                dst_ref=halves[k].at[g, hop - 1],
                send_sem=rs_send.at[g, slots[k] + hop - 1],
                recv_sem=rs_recv.at[g, slots[k] + hop - 1],
                device_id={"gx": partner},
                device_id_type=MESH,
            )
            copy.start()
            copies.append(copy)
        flying[g] = copies
        if shares:
            starts[g] = starts[g] + mine * rows

    def reduce_end(g, k):
        distance, radix, rows, shares = stages[k]
        for copy in flying[g]:
            copy.wait_recv()
            if shares:
                pending.append(copy)
            else:
                copy.wait_send()
        at = rows_at(starts[g], rows)
        held = [stats[:, at, :].astype(F32)]
        held += [halves[k][g, hop].astype(F32) for hop in range(radix - 1)]
        peak = functools.reduce(jnp.maximum, [each[0] for each in held])
        scales = [jnp.exp(each[0] - peak) for each in held]
        norm = sum(each[1] * scale for each, scale in zip(held, scales))
        total = sum(each[2] * scale for each, scale in zip(held, scales))
        if k + 1 < len(stages):
            stats[:, at, :] = jnp.stack([peak, norm, total]).astype(BF16)
        else:
            pooled[rows_at(PAD + starts[g], rows), :] = (total / norm).astype(BF16)

    def gather_copy(g, slot, start, rows, partner):
        part = pooled.at[rows_at(PAD + start, rows), :]
        copy = pltpu.make_async_remote_copy(
            src_ref=part,
            dst_ref=part,
            send_sem=ag_send.at[g, slot],
            recv_sem=ag_recv.at[g, slot],
            device_id={"gx": partner},
            device_id_type=MESH,
        )
        copy.start()
        pending.append(copy)
        return copy

    def gather_far(g):
        rows = stages[-1][2]
        flying[g] = [
            gather_copy(g, i, starts[g], rows, partner) for i, partner in enumerate(far)
        ]

    def gather_near(g):
        for copy in flying[g]:
            copy.wait_recv()
        rows = stages[0][2]
        flying[g] = [
            gather_copy(g, len(far), g * tile + digits[0] * rows, rows, partners[0][1][0])
        ]

    def gather_end(g):
        for copy in flying[g]:
            copy.wait_recv()

    def strip_copy(side):
        return pltpu.make_async_remote_copy(
            src_ref=strip.at[1 + side],
            dst_ref=strip.at[3 - 3 * side],
            send_sem=strip_send.at[side],
            recv_sem=strip_recv.at[1 - side],
            device_id={"gx": (left, right)[side]},
            device_id_type=MESH,
        )

    def strip_start():
        for side, has in ((0, has_left), (1, has_right)):
            _, norm, total = running[side]
            strip[1 + side] = (total / norm).astype(BF16).astype(F32)

            @pl.when(has)
            def _():
                strip_copy(side).start()

    def strip_plane():
        for side, has in ((0, has_left), (1, has_right)):

            @pl.when(has)
            def _():
                strip_copy(1 - side).wait_recv()

        rows_z = [shifted(strip[i], depth) for i in range(4)]
        stacked = [
            jnp.concatenate([part for i in range(3) for part in rows_z[x + i]], axis=1)
            for x in range(2)
        ]
        plane = dot(jnp.concatenate(stacked, axis=0).astype(BF16), w_xz[...])
        return plane.astype(BF16).astype(F32)

    def finish(t):
        at = slice(t * tile, (t + 1) * tile)
        plane_yz = dot(neighbourhood(pooled, t * tile, tile, depth), w_yz[...])
        plane_yz = plane_yz.astype(BF16).astype(F32).reshape(cells, depth, channels)
        for side in range(2):
            mixing = plane_yz + plane_xz[side * depth : (side + 1) * depth][None]
            joined = feature[side, at, :].astype(F32) * mixing.reshape(tile, channels)
            scale = lax.rsqrt(jnp.mean(joined * joined, axis=-1, keepdims=True) + 1e-06)
            normed = (joined * scale * norm_gain[...]).astype(BF16)
            hidden = activate(dot(normed, w_in[...])).astype(BF16)
            out[side, at, :] = (joined + dot(hidden, w_out[...])).astype(BF16)

    last = len(stages)
    plane_xz = None
    for slot in range(tiles + last + 3):
        if slot < tiles:
            local_part(slot)
        if slot == tiles - 1:
            strip_start()
        for g in range(tiles):
            step = slot - g
            if 1 <= step <= last:
                reduce_end(g, step - 1)
            if 0 <= step < last:
                reduce_start(g, step)
            if step == last:
                gather_far(g)
            if step == last + 1:
                gather_near(g)
            if step == last + 2:
                gather_end(g)
        if slot == tiles:
            plane_xz = strip_plane()
        ready = slot - last - 3
        if 0 <= ready < tiles:
            finish(ready)

    for copy in pending:
        copy.wait_send()
    sent(vox_copy)
    sent(first_copy)
    for side, has in ((0, has_left), (1, has_right)):

        @pl.when(has)
        def _():
            strip_copy(side).wait_send()


def on_device(
    n,
    voxels,
    prior,
    conv_first,
    conv_second,
    score_x,
    score_y,
    plane_yz_w,
    plane_xz_w,
    norm_gain,
    mlp_in,
    mlp_out,
):
    rows, across, depth, channels = voxels.shape
    assert rows == 2 and depth == 8 and n & (n - 1) == 0
    length = across * depth
    hidden = mlp_in.shape[1]
    tile = min(256, length)
    tiles = length // tile
    stages = stages_of(tile, n)
    exchanges = sum(stage[1] - 1 for stage in stages)
    padded = length + 2 * PAD
    taps = conv_first.shape[0] // 3 * channels
    hbm = pl.BlockSpec(memory_space=pl.ANY)
    vmem = pl.BlockSpec(memory_space=pltpu.VMEM)
    result = pl.pallas_call(
        functools.partial(kernel, n, tile, stages),
        out_shape=jax.ShapeDtypeStruct((rows, length, channels), BF16),
        in_specs=[hbm, vmem, hbm, hbm, hbm, hbm, hbm, hbm, vmem, hbm, hbm],
        out_specs=vmem,
        scratch_shapes=[
            pltpu.VMEM((taps, 3 * channels), BF16),
            pltpu.VMEM((taps, 3 * channels), BF16),
            pltpu.VMEM((channels, 2 * channels), BF16),
            pltpu.VMEM((taps, channels), BF16),
            pltpu.VMEM((taps, channels), BF16),
            pltpu.VMEM((channels, hidden), BF16),
            pltpu.VMEM((hidden, channels), BF16),
            pltpu.VMEM((2, padded, channels), BF16),
            pltpu.VMEM((2, padded, channels), BF16),
            pltpu.VMEM((2, padded, channels), BF16),
            pltpu.VMEM((2, padded, channels), BF16),
            pltpu.VMEM((length, 2 * channels), F32),
            pltpu.VMEM((2, length, channels), BF16),
            pltpu.VMEM((3, length, channels), BF16),
            pltpu.VMEM((padded, channels), BF16),
            pltpu.VMEM((4, depth, channels), F32),
            [
                pltpu.VMEM((tiles, radix - 1, 3, share, channels), BF16)
                for _, radix, share, _ in stages
            ],
            pltpu.SemaphoreType.DMA((12,)),
            pltpu.SemaphoreType.DMA((2,)),
            pltpu.SemaphoreType.DMA((2, 2, tiles)),
            pltpu.SemaphoreType.DMA((2, 2, tiles)),
            pltpu.SemaphoreType.DMA((2,)),
            pltpu.SemaphoreType.DMA((2,)),
            pltpu.SemaphoreType.DMA((tiles, exchanges)),
            pltpu.SemaphoreType.DMA((tiles, exchanges)),
            pltpu.SemaphoreType.DMA((tiles, far_radix(stages))),
            pltpu.SemaphoreType.DMA((tiles, far_radix(stages))),
        ],
        compiler_params=pltpu.CompilerParams(
            collective_id=0, has_side_effects=True, vmem_limit_bytes=62 * 1024 * 1024
        ),
    )(
        voxels.reshape(rows, length, channels),
        prior.transpose(0, 2, 1),
        conv_first.reshape(3, taps, channels),
        conv_second.reshape(3, taps, channels),
        score_x,
        score_y,
        plane_yz_w.reshape(taps, channels),
        plane_xz_w.reshape(taps, channels),
        norm_gain.reshape(1, channels),
        mlp_in,
        mlp_out,
    )
    return result.reshape(voxels.shape)


def solution(mesh):
    split = P(("scene", "gx"), None, None, None)
    return jax.shard_map(
        functools.partial(on_device, mesh.shape["gx"]),
        mesh=mesh,
        in_specs=(split, P(("scene", "gx"), None, None)) + (P(),) * 9,
        out_specs=split,
        check_vma=False,
    )
```

```python
import functools

import jax
import jax.numpy as jnp
from jax import lax
from jax.experimental import pallas as pl
from jax.experimental.pallas import tpu as pltpu
from jax.sharding import PartitionSpec as P

MESH = pl.DeviceIdType.MESH
PAD = 16
F32 = jnp.float32
BF16 = jnp.bfloat16


def activate(values):
    return jax.nn.gelu(values, approximate=True)


def stages_of(rows, devices):
    count = devices.bit_length() - 1
    bits = [[i] for i in range(min(2, count))]
    bits += [list(range(i, min(i + 2, count))) for i in range(2, count, 2)]
    stages = []
    for group in bits:
        radix = 1 << len(group)
        shares = rows % (16 * radix) == 0
        rows = rows // radix if shares else rows
        stages.append((1 << group[0], radix, rows, shares))
    return stages


def far_radix(stages):
    total = 1
    for distance, radix, _, shares in stages:
        if shares and distance > 1:
            total *= radix
    return total


def shifted(values):
    depth = values.shape[1]
    at_z = lax.broadcasted_iota(jnp.int32, (1,) + values.shape[1:], 1)
    below = jnp.where(at_z == 0, 0.0, pltpu.roll(values, 1, 1))
    above = jnp.where(at_z == depth - 1, 0.0, pltpu.roll(values, depth - 1, 1))
    return below, values, above


def stack(source, even, odd, start, rows, depth):
    channels = source.shape[1]
    window = source[pl.ds(pl.multiple_of(start - PAD, 16), rows + PAD), :].astype(F32)
    parts = shifted(window.reshape(-1, depth, channels))
    at = pl.ds(pl.multiple_of(start, 16), rows)
    for i, part in enumerate(parts):
        part = part.reshape(rows + PAD, channels)
        columns = slice(i * channels, (i + 1) * channels)
        even[at, columns] = part[PAD:].astype(BF16)
        odd[at, columns] = part[PAD - depth : rows + PAD - depth].astype(BF16)


def neighbourhood(even, odd, start, tile):
    first = pl.ds(pl.multiple_of(start, 16), tile)
    after = pl.ds(pl.multiple_of(start + PAD, 16), tile)
    return jnp.concatenate([odd[first, :], even[first, :], odd[after, :]], axis=1)


def dot(a, b):
    return jnp.dot(a, b, preferred_element_type=F32)


def kernel(
    n,
    tile,
    stages,
    voxels,
    prior,
    conv_first,
    conv_second,
    score_x,
    score_y,
    plane_yz_w,
    plane_xz_w,
    norm_gain,
    mlp_in,
    mlp_out,
    out,
    w_first,
    w_second,
    w_score,
    w_yz,
    w_xz,
    w_in,
    w_out,
    vox,
    face_vox,
    first,
    face_first,
    acc,
    feature,
    stats,
    pooled,
    strip,
    running,
    plane_xz,
    even,
    odd,
    halves,
    load_sem,
    vox_sem,
    face_send,
    face_recv,
    strip_send,
    strip_recv,
    rs_send,
    rs_recv,
    ag_send,
    ag_recv,
):
    me = lax.axis_index("gx")
    length, channels = voxels.shape[1], voxels.shape[2]
    depth = prior.shape[1]
    tiles = length // tile
    has_left, has_right = me > 0, me < n - 1
    left, right = me - 1, me + 1
    across = length // depth

    def across_bits(distance, hop):
        other, weight = me, 1
        while weight <= hop:
            bit = (me // (distance * weight)) % 2
            if hop & weight:
                other = other + (1 - 2 * bit) * distance * weight
            weight *= 2
        return other

    digits = [(me // distance) % radix for distance, radix, _, _ in stages]
    partners = []
    for distance, radix, _, _ in stages:
        found = {}
        for hop in range(1, radix):
            other = across_bits(distance, hop)
            found[hop] = (other, (other // distance) % radix)
        partners.append(found)
    slots = [sum(stage[1] - 1 for stage in stages[:k]) for k in range(len(stages))]
    far = [across_bits(2, hop) for hop in range(1, far_radix(stages))]

    loads = [
        (conv_first.at[tap], w_first.at[:, pl.ds((2 - tap) * channels, channels)]) for tap in range(3)
    ]
    loads += [
        (conv_second.at[tap], w_second.at[:, pl.ds((2 - tap) * channels, channels)])
        for tap in range(3)
    ]
    loads += [
        (score_x, w_score.at[:, pl.ds(0, channels)]),
        (score_y, w_score.at[:, pl.ds(channels, channels)]),
        (plane_yz_w, w_yz),
        (plane_xz_w, w_xz),
        (mlp_in, w_in),
        (mlp_out, w_out),
    ]
    vox_loads = [
        pltpu.make_async_copy(
            voxels.at[row], vox.at[row, pl.ds(PAD, length), :], vox_sem.at[row]
        )
        for row in range(2)
    ]
    loads = [
        pltpu.make_async_copy(source, target, load_sem.at[i])
        for i, (source, target) in enumerate(loads)
    ]
    for copy in vox_loads + loads:
        copy.start()

    barrier = pltpu.get_barrier_semaphore()
    greeted = far + [
        partner
        for stage, found in zip(stages, partners)
        for partner, _ in found.values()
        if stage[0] == 1 or not stage[3]
    ]
    for partner in greeted:
        pl.semaphore_signal(barrier, inc=1, device_id={"gx": partner}, device_id_type=MESH)

    @pl.when(has_left)
    def _():
        pl.semaphore_signal(barrier, inc=1, device_id={"gx": left}, device_id_type=MESH)

    @pl.when(has_right)
    def _():
        pl.semaphore_signal(barrier, inc=1, device_id={"gx": right}, device_id_type=MESH)

    edge = jnp.zeros((2, PAD, channels), BF16)
    for padded in (vox, face_vox, first, face_first):
        padded[:, 0:PAD, :] = edge
        padded[:, PAD + length :, :] = edge
    pooled[0:PAD, :] = edge[0]
    pooled[PAD + length :, :] = edge[0]

    for side, has in ((0, has_left), (1, has_right)):

        @pl.when(jnp.logical_not(has))
        def _():
            blank = jnp.zeros((length, channels), BF16)
            face_vox[side, pl.ds(PAD, length), :] = blank
            face_first[side, pl.ds(PAD, length), :] = blank
            strip[3 * side] = jnp.zeros(strip.shape[1:], F32)

    pl.semaphore_wait(barrier, len(greeted) + jnp.where(has_left, 1, 0) + jnp.where(has_right, 1, 0))

    def face_copy(which, source, target, side, t, to):
        return pltpu.make_async_remote_copy(
            src_ref=source,
            dst_ref=target.at[1 - side, pl.ds(pl.multiple_of(PAD + t * tile, 16), tile), :],
            send_sem=face_send.at[which, side, t],
            recv_sem=face_recv.at[which, 1 - side, t],
            device_id={"gx": to},
            device_id_type=MESH,
        )

    def vox_copy(side, t):
        source = voxels.at[side, pl.ds(pl.multiple_of(t * tile, 16), tile), :]
        return face_copy(0, source, face_vox, side, t, (left, right)[side])

    def first_copy(side, t):
        source = first.at[side, pl.ds(pl.multiple_of(PAD + t * tile, 16), tile), :]
        return face_copy(1, source, face_first, side, t, (left, right)[side])

    def arrive(make, side, t, has):
        @pl.when(has)
        def _():
            make(1 - side, t).wait_recv()

    def sent(make):
        for side, has in ((0, has_left), (1, has_right)):

            @pl.when(has)
            def _():
                for t in range(tiles):
                    make(side, t).wait_send()

    for t in range(tiles):
        for side, has in ((0, has_left), (1, has_right)):

            @pl.when(has)
            def _():
                vox_copy(side, t).start()

    def stack_tile(layer, source, t):
        stack(source, even.at[layer], odd.at[layer], PAD + t * tile, tile, depth)

    def stack_end(layer, source):
        stack(source, even.at[layer], odd.at[layer], PAD + length, PAD, depth)

    def around(layer, t):
        return neighbourhood(even.at[layer], odd.at[layer], PAD + t * tile, tile)

    def tile_at(t, offset=0):
        return pl.ds(pl.multiple_of(offset + t * tile, 16), tile)

    def inner(base, weight, t):
        total = dot(around(base, t), weight[:, channels:])
        total += dot(around(base + 1, t), weight[:, : 2 * channels])
        acc[tile_at(t), :] = total

    def face_tile(base, face, make, t):
        for side, has in ((0, has_left), (1, has_right)):
            arrive(make, side, t, has)
            stack_tile(base + 2 + side, face.at[side], t)

    def outer(base, weight, side, t):
        low = 2 * channels * (1 - side)
        return acc[tile_at(t), side * channels : (side + 1) * channels] + dot(
            around(base + 2 + side, t), weight[:, low : low + channels]
        )

    def repeat(count, body):
        def step(t, carry):
            body(t)
            return carry

        lax.fori_loop(0, count, step, 0)

    for copy in vox_loads + loads[:3]:
        copy.wait()

    @functools.partial(repeat, tiles + 1)
    def _(t):
        @pl.when(t < tiles)
        def _():
            for side in range(2):
                stack_tile(side, vox.at[side], t)

        @pl.when(t == tiles)
        def _():
            for side in range(2):
                stack_end(side, vox.at[side])

        @pl.when(t >= 1)
        def _():
            inner(0, w_first, t - 1)

    for copy in loads[3:]:
        copy.wait()

    @functools.partial(repeat, tiles + 2)
    def _(t):
        @pl.when(t < tiles)
        def _():
            face_tile(0, face_vox, vox_copy, t)

        @pl.when(t == tiles)
        def _():
            for side in range(2):
                stack_end(2 + side, face_vox.at[side])

        @pl.when(jnp.logical_and(t >= 1, t <= tiles))
        def _():
            u = t - 1
            for side, has in ((0, has_left), (1, has_right)):
                value = activate(outer(0, w_first, side, u)).astype(BF16)
                first[side, tile_at(u, PAD), :] = value

                @pl.when(has)
                def _():
                    first_copy(side, u).start()

            for side in range(2):
                stack_tile(4 + side, first.at[side], u)

        @pl.when(t == tiles)
        def _():
            for side in range(2):
                stack_end(4 + side, first.at[side])

        @pl.when(t >= 2)
        def _():
            inner(4, w_second, t - 2)

    cells = tile // depth
    cube = (cells, depth, across)
    running[:, 0] = jnp.full((2, depth, channels), -jnp.inf, F32)
    running[:, 1:] = jnp.zeros((2, 2, depth, channels), F32)

    def local_part(t):
        logits, features = [], []
        lane = lax.broadcasted_iota(jnp.int32, cube, 2)
        cell = lax.broadcasted_iota(jnp.int32, cube, 0) + t * cells
        for side in range(2):
            value = outer(4, w_second, side, t)
            value += vox[side, tile_at(t, PAD), :].astype(F32)
            value = value.astype(BF16)
            feature[side, tile_at(t), :] = value
            both = dot(value, w_score[...])
            field = jnp.broadcast_to(prior[side][None], cube)
            field = jnp.where(lane == cell, field, 0.0)
            field = jnp.sum(field, axis=2, keepdims=True)
            field = jnp.broadcast_to(field, (cells, depth, channels))
            value = value.astype(F32)
            logits.append(both[:, :channels] + field.reshape(tile, channels))
            features.append(value)
            logit_y = both[:, channels:].reshape(cells, depth, channels) + field
            value = value.reshape(cells, depth, channels)
            old, norm, total = running[side, 0], running[side, 1], running[side, 2]
            peak = jnp.maximum(jnp.max(logit_y, axis=0), old)
            weight = jnp.exp(logit_y - peak[None])
            keep = jnp.exp(old - peak)
            running[side, 0] = peak
            running[side, 1] = norm * keep + jnp.sum(weight, 0)
            running[side, 2] = total * keep + jnp.sum(weight * value, 0)
        peak = jnp.maximum(logits[0], logits[1]).astype(BF16)
        weights = [jnp.exp(logit - peak.astype(F32)) for logit in logits]
        stats[0, tile_at(t), :] = peak
        stats[1, tile_at(t), :] = (weights[0] + weights[1]).astype(BF16)
        stats[2, tile_at(t), :] = (weights[0] * features[0] + weights[1] * features[1]).astype(BF16)

    def rows_at(start, rows):
        return pl.ds(pl.multiple_of(start, 16), rows)

    def start_of(g, k):
        start = g * tile
        for digit, (_, _, rows, shares) in zip(digits[:k], stages):
            if shares:
                start = start + digit * rows
        return start

    def reduce_copies(g, k):
        distance, radix, rows, shares = stages[k]
        copies = []
        for hop in range(1, radix):
            partner, theirs = partners[k][hop]
            give = start_of(g, k)
            if shares:
                give = give + theirs * rows
            copies.append(
                pltpu.make_async_remote_copy(
                    src_ref=stats.at[:, rows_at(give, rows), :],
                    dst_ref=halves[k].at[g, hop - 1],
                    send_sem=rs_send.at[g, slots[k] + hop - 1],
                    recv_sem=rs_recv.at[g, slots[k] + hop - 1],
                    device_id={"gx": partner},
                    device_id_type=MESH,
                )
            )
        return copies

    def reduce_end(g, k):
        distance, radix, rows, shares = stages[k]
        for copy in reduce_copies(g, k):
            copy.wait_recv()
            if not shares:
                copy.wait_send()
        start = start_of(g, k + 1)
        at = rows_at(start, rows)
        held = [stats[:, at, :].astype(F32)]
        held += [halves[k][g, hop].astype(F32) for hop in range(radix - 1)]
        peak = functools.reduce(jnp.maximum, [each[0] for each in held])
        scales = [jnp.exp(each[0] - peak) for each in held]
        norm = sum(each[1] * scale for each, scale in zip(held, scales))
        total = sum(each[2] * scale for each, scale in zip(held, scales))
        if k + 1 < len(stages):
            for i, value in enumerate((peak, norm, total)):
                stats[i, at, :] = value.astype(BF16)
        else:
            pooled[rows_at(PAD + start, rows), :] = (total / norm).astype(BF16)

    def gather_copy(g, slot, start, rows, partner):
        part = pooled.at[rows_at(PAD + start, rows), :]
        return pltpu.make_async_remote_copy(
            src_ref=part,
            dst_ref=part,
            send_sem=ag_send.at[g, slot],
            recv_sem=ag_recv.at[g, slot],
            device_id={"gx": partner},
            device_id_type=MESH,
        )

    def far_copies(g):
        start, rows = start_of(g, len(stages)), stages[-1][2]
        return [gather_copy(g, i, start, rows, partner) for i, partner in enumerate(far)]

    def near_copies(g):
        rows = stages[0][2]
        return [gather_copy(g, len(far), start_of(g, 1), rows, partners[0][1][0])]

    def strip_copy(side):
        return pltpu.make_async_remote_copy(
            src_ref=strip.at[1 + side],
            dst_ref=strip.at[3 - 3 * side],
            send_sem=strip_send.at[side],
            recv_sem=strip_recv.at[1 - side],
            device_id={"gx": (left, right)[side]},
            device_id_type=MESH,
        )

    def strip_start():
        for side, has in ((0, has_left), (1, has_right)):
            strip[1 + side] = (running[side, 2] / running[side, 1]).astype(BF16).astype(F32)

            @pl.when(has)
            def _():
                strip_copy(side).start()

    def strip_plane():
        for side, has in ((0, has_left), (1, has_right)):

            @pl.when(has)
            def _():
                strip_copy(1 - side).wait_recv()

        moved = shifted(strip[...])
        stacked = [
            jnp.concatenate([part[x + i] for i in range(3) for part in moved], axis=1)
            for x in range(2)
        ]
        plane = dot(jnp.concatenate(stacked, axis=0).astype(BF16), w_xz[...])
        plane_xz[...] = plane.astype(BF16).astype(F32)

    def finish(t):
        plane_yz = dot(around(8, t), w_yz[...])
        plane_yz = plane_yz.astype(BF16).astype(F32).reshape(cells, depth, channels)
        for side in range(2):
            mixing = plane_yz + plane_xz[side * depth : (side + 1) * depth, :][None]
            joined = feature[side, tile_at(t), :].astype(F32) * mixing.reshape(tile, channels)
            scale = lax.rsqrt(jnp.mean(joined * joined, axis=-1, keepdims=True) + 1e-06)
            normed = (joined * scale * norm_gain[...]).astype(BF16)
            hidden = activate(dot(normed, w_in[...])).astype(BF16)
            out[side, tile_at(t), :] = (joined + dot(hidden, w_out[...])).astype(BF16)

    last = len(stages)

    @functools.partial(repeat, tiles + last + 4)
    def _(slot):
        @pl.when(slot < tiles)
        def _():
            face_tile(4, face_first, first_copy, slot)

        @pl.when(slot == tiles)
        def _():
            for side in range(2):
                stack_end(6 + side, face_first.at[side])

        @pl.when(jnp.logical_and(slot >= 1, slot <= tiles))
        def _():
            local_part(slot - 1)

        def at_step(step, body):
            g = slot - 1 - step

            @pl.when(jnp.logical_and(g >= 0, g < tiles))
            def _():
                body(g)

        def start_all(copies):
            for copy in copies:
                copy.start()

        def end_all(copies):
            for copy in copies:
                copy.wait_recv()

        def advance(k, g):
            if k > 0:
                reduce_end(g, k - 1)
            start_all(reduce_copies(g, k) if k < last else far_copies(g))

        def gather_near(g):
            end_all(far_copies(g))
            start_all(near_copies(g))

        def gather_end(g):
            end_all(near_copies(g))
            stack_tile(8, pooled, g)

            @pl.when(g == tiles - 1)
            def _():
                stack_end(8, pooled)

        for k in range(last + 1):
            at_step(k, functools.partial(advance, k))
        at_step(last + 1, gather_near)
        at_step(last + 2, gather_end)

        @pl.when(slot == tiles)
        def _():
            strip_start()

        @pl.when(slot == tiles + 1)
        def _():
            strip_plane()

        at_step(last + 3, finish)

    @functools.partial(repeat, tiles)
    def _(g):
        for k, (_, _, _, shares) in enumerate(stages):
            for copy in reduce_copies(g, k) if shares else []:
                copy.wait_send()
        for copy in far_copies(g) + near_copies(g):
            copy.wait_send()

    sent(vox_copy)
    sent(first_copy)
    for side, has in ((0, has_left), (1, has_right)):

        @pl.when(has)
        def _():
            strip_copy(side).wait_send()


def on_device(
    n,
    voxels,
    prior,
    conv_first,
    conv_second,
    score_x,
    score_y,
    plane_yz_w,
    plane_xz_w,
    norm_gain,
    mlp_in,
    mlp_out,
):
    rows, across, depth, channels = voxels.shape
    assert rows == 2 and depth == 8 and n & (n - 1) == 0
    length = across * depth
    hidden = mlp_in.shape[1]
    tile = min(256, length)
    tiles = length // tile
    stages = stages_of(tile, n)
    exchanges = sum(stage[1] - 1 for stage in stages)
    padded = length + 2 * PAD
    taps = conv_first.shape[0] // 3 * channels
    hbm = pl.BlockSpec(memory_space=pl.ANY)
    vmem = pl.BlockSpec(memory_space=pltpu.VMEM)
    result = pl.pallas_call(
        functools.partial(kernel, n, tile, stages),
        out_shape=jax.ShapeDtypeStruct((rows, length, channels), BF16),
        in_specs=[hbm, vmem, hbm, hbm, hbm, hbm, hbm, hbm, vmem, hbm, hbm],
        out_specs=vmem,
        scratch_shapes=[
            pltpu.VMEM((taps, 3 * channels), BF16),
            pltpu.VMEM((taps, 3 * channels), BF16),
            pltpu.VMEM((channels, 2 * channels), BF16),
            pltpu.VMEM((taps, channels), BF16),
            pltpu.VMEM((taps, channels), BF16),
            pltpu.VMEM((channels, hidden), BF16),
            pltpu.VMEM((hidden, channels), BF16),
            pltpu.VMEM((2, padded, channels), BF16),
            pltpu.VMEM((2, padded, channels), BF16),
            pltpu.VMEM((2, padded, channels), BF16),
            pltpu.VMEM((2, padded, channels), BF16),
            pltpu.VMEM((length, 2 * channels), F32),
            pltpu.VMEM((2, length, channels), BF16),
            pltpu.VMEM((3, length, channels), BF16),
            pltpu.VMEM((padded, channels), BF16),
            pltpu.VMEM((4, depth, channels), F32),
            pltpu.VMEM((2, 3, depth, channels), F32),
            pltpu.VMEM((2 * depth, channels), F32),
            pltpu.VMEM((9, padded, 3 * channels), BF16),
            pltpu.VMEM((9, padded, 3 * channels), BF16),
            [
                pltpu.VMEM((tiles, radix - 1, 3, share, channels), BF16)
                for _, radix, share, _ in stages
            ],
            pltpu.SemaphoreType.DMA((12,)),
            pltpu.SemaphoreType.DMA((2,)),
            pltpu.SemaphoreType.DMA((2, 2, tiles)),
            pltpu.SemaphoreType.DMA((2, 2, tiles)),
            pltpu.SemaphoreType.DMA((2,)),
            pltpu.SemaphoreType.DMA((2,)),
            pltpu.SemaphoreType.DMA((tiles, exchanges)),
            pltpu.SemaphoreType.DMA((tiles, exchanges)),
            pltpu.SemaphoreType.DMA((tiles, far_radix(stages))),
            pltpu.SemaphoreType.DMA((tiles, far_radix(stages))),
        ],
        compiler_params=pltpu.CompilerParams(
            collective_id=0, has_side_effects=True, vmem_limit_bytes=62 * 1024 * 1024
        ),
    )(
        voxels.reshape(rows, length, channels),
        prior.transpose(0, 2, 1),
        conv_first.reshape(3, taps, channels),
        conv_second.reshape(3, taps, channels),
        score_x,
        score_y,
        plane_yz_w.reshape(taps, channels),
        plane_xz_w.reshape(taps, channels),
        norm_gain.reshape(1, channels),
        mlp_in,
        mlp_out,
    )
    return result.reshape(voxels.shape)


def solution(mesh):
    split = P(("scene", "gx"), None, None, None)
    return jax.shard_map(
        functools.partial(on_device, mesh.shape["gx"]),
        mesh=mesh,
        in_specs=(split, P(("scene", "gx"), None, None)) + (P(),) * 9,
        out_specs=split,
        check_vma=False,
    )
```

```python
import functools

import jax
import jax.numpy as jnp
from jax import lax
from jax.experimental import pallas as pl
from jax.experimental.pallas import tpu as pltpu
from jax.sharding import PartitionSpec as P

MESH = pl.DeviceIdType.MESH
PAD = 16
F32 = jnp.float32
BF16 = jnp.bfloat16


def activate(values):
    return jax.nn.gelu(values, approximate=True)


def stages_of(rows, devices):
    count = devices.bit_length() - 1
    bits = [[i] for i in range(min(2, count))]
    bits += [list(range(i, min(i + 2, count))) for i in range(2, count, 2)]
    stages = []
    for group in bits:
        radix = 1 << len(group)
        shares = rows % (16 * radix) == 0
        rows = rows // radix if shares else rows
        stages.append((1 << group[0], radix, rows, shares))
    return stages


def far_radix(stages):
    total = 1
    for distance, radix, _, shares in stages:
        if shares and distance > 1:
            total *= radix
    return total


def shifted(values):
    depth = values.shape[1]
    at_z = lax.broadcasted_iota(jnp.int32, (1,) + values.shape[1:], 1)
    below = jnp.where(at_z == 0, 0.0, pltpu.roll(values, 1, 1))
    above = jnp.where(at_z == depth - 1, 0.0, pltpu.roll(values, depth - 1, 1))
    return below, values, above


def stack(source, even, odd, start, rows, depth):
    channels = source.shape[1]
    window = source[pl.ds(pl.multiple_of(start - PAD, 16), rows + PAD), :].astype(F32)
    parts = shifted(window.reshape(-1, depth, channels))
    at = pl.ds(pl.multiple_of(start, 16), rows)
    for i, part in enumerate(parts):
        part = part.reshape(rows + PAD, channels)
        columns = slice(i * channels, (i + 1) * channels)
        even[at, columns] = part[PAD:].astype(BF16)
        odd[at, columns] = part[PAD - depth : rows + PAD - depth].astype(BF16)


def neighbourhood(even, odd, start, tile):
    first = pl.ds(pl.multiple_of(start, 16), tile)
    after = pl.ds(pl.multiple_of(start + PAD, 16), tile)
    return jnp.concatenate([odd[first, :], even[first, :], odd[after, :]], axis=1)


def dot(a, b):
    return jnp.dot(a, b, preferred_element_type=F32)


def kernel(
    n,
    tile,
    stages,
    voxels,
    prior,
    conv_first,
    conv_second,
    score_x,
    score_y,
    plane_yz_w,
    plane_xz_w,
    norm_gain,
    mlp_in,
    mlp_out,
    out,
    w_first,
    w_second,
    w_score,
    w_yz,
    w_xz,
    w_in,
    w_out,
    vox,
    face_vox,
    first,
    face_first,
    acc,
    feature,
    stats,
    pooled,
    strip,
    running,
    plane_xz,
    spread,
    even,
    odd,
    halves,
    load_sem,
    vox_sem,
    face_send,
    face_recv,
    strip_send,
    strip_recv,
    rs_send,
    rs_recv,
    ag_send,
    ag_recv,
):
    me = lax.axis_index("gx")
    length, channels = voxels.shape[1], voxels.shape[2]
    depth = prior.shape[1]
    tiles = length // tile
    has_left, has_right = me > 0, me < n - 1
    left, right = me - 1, me + 1
    across = length // depth

    def across_bits(distance, hop):
        other, weight = me, 1
        while weight <= hop:
            bit = (me // (distance * weight)) % 2
            if hop & weight:
                other = other + (1 - 2 * bit) * distance * weight
            weight *= 2
        return other

    digits = [(me // distance) % radix for distance, radix, _, _ in stages]
    partners = []
    for distance, radix, _, _ in stages:
        found = {}
        for hop in range(1, radix):
            other = across_bits(distance, hop)
            found[hop] = (other, (other // distance) % radix)
        partners.append(found)
    slots = [sum(stage[1] - 1 for stage in stages[:k]) for k in range(len(stages))]
    far = [across_bits(2, hop) for hop in range(1, far_radix(stages))]

    taps = conv_first.shape[1]
    loads = []
    for source, target in ((conv_first, w_first), (conv_second, w_second)):
        for layer in range(2):
            for result in range(2):
                block = (pl.ds(layer * taps, taps), pl.ds(result * channels, channels))
                loads.append((source.at[1 + layer - result], target.at[block]))
    loads += [
        (score_x, w_score.at[:, pl.ds(0, channels)]),
        (score_y, w_score.at[:, pl.ds(channels, channels)]),
        (plane_yz_w, w_yz),
        (plane_xz_w, w_xz),
        (mlp_in, w_in),
        (mlp_out, w_out),
    ]
    vox_loads = [
        pltpu.make_async_copy(
            voxels.at[row], vox.at[row, pl.ds(PAD, length), :], vox_sem.at[row]
        )
        for row in range(2)
    ]
    loads = [
        pltpu.make_async_copy(source, target, load_sem.at[i])
        for i, (source, target) in enumerate(loads)
    ]
    for copy in vox_loads + loads:
        copy.start()

    barrier = pltpu.get_barrier_semaphore()
    greeted = far + [
        partner
        for stage, found in zip(stages, partners)
        for partner, _ in found.values()
        if stage[0] == 1 or not stage[3]
    ]
    for partner in greeted:
        pl.semaphore_signal(barrier, inc=1, device_id={"gx": partner}, device_id_type=MESH)

    @pl.when(has_left)
    def _():
        pl.semaphore_signal(barrier, inc=1, device_id={"gx": left}, device_id_type=MESH)

    @pl.when(has_right)
    def _():
        pl.semaphore_signal(barrier, inc=1, device_id={"gx": right}, device_id_type=MESH)

    edge = jnp.zeros((2, PAD, channels), BF16)
    for padded in (vox, face_vox, first, face_first):
        padded[:, 0:PAD, :] = edge
        padded[:, PAD + length :, :] = edge
    pooled[0:PAD, :] = edge[0]
    pooled[PAD + length :, :] = edge[0]

    for side, has in ((0, has_left), (1, has_right)):

        @pl.when(jnp.logical_not(has))
        def _():
            blank = jnp.zeros((length, channels), BF16)
            face_vox[side, pl.ds(PAD, length), :] = blank
            face_first[side, pl.ds(PAD, length), :] = blank
            strip[3 * side] = jnp.zeros(strip.shape[1:], F32)

    pl.semaphore_wait(barrier, len(greeted) + jnp.where(has_left, 1, 0) + jnp.where(has_right, 1, 0))

    def face_copy(which, source, target, side, t, to):
        return pltpu.make_async_remote_copy(
            src_ref=source,
            dst_ref=target.at[1 - side, pl.ds(pl.multiple_of(PAD + t * tile, 16), tile), :],
            send_sem=face_send.at[which, side, t],
            recv_sem=face_recv.at[which, 1 - side, t],
            device_id={"gx": to},
            device_id_type=MESH,
        )

    def vox_copy(side, t):
        source = voxels.at[side, pl.ds(pl.multiple_of(t * tile, 16), tile), :]
        return face_copy(0, source, face_vox, side, t, (left, right)[side])

    def first_copy(side, t):
        source = first.at[side, pl.ds(pl.multiple_of(PAD + t * tile, 16), tile), :]
        return face_copy(1, source, face_first, side, t, (left, right)[side])

    def arrive(make, side, t, has):
        @pl.when(has)
        def _():
            make(1 - side, t).wait_recv()

    def sent(make):
        for side, has in ((0, has_left), (1, has_right)):

            @pl.when(has)
            def _():
                for t in range(tiles):
                    make(side, t).wait_send()

    for t in range(tiles):
        for side, has in ((0, has_left), (1, has_right)):

            @pl.when(has)
            def _():
                vox_copy(side, t).start()

    def stack_tile(layer, source, t):
        stack(source, even.at[layer], odd.at[layer], PAD + t * tile, tile, depth)

    def stack_end(layer, source):
        stack(source, even.at[layer], odd.at[layer], PAD + length, PAD, depth)

    def around(layer, t):
        return neighbourhood(even.at[layer], odd.at[layer], PAD + t * tile, tile)

    def tile_at(t, offset=0):
        return pl.ds(pl.multiple_of(offset + t * tile, 16), tile)

    def inner(base, weight, t):
        both = jnp.concatenate([around(base, t), around(base + 1, t)], axis=1)
        acc[tile_at(t), :] = dot(both, weight[...])

    def face_tile(base, face, make, t):
        for side, has in ((0, has_left), (1, has_right)):
            arrive(make, side, t, has)
            stack_tile(base + 2 + side, face.at[side], t)

    def outer(base, weight, side, t):
        if side == 0:
            part = weight[:taps, channels:]
        else:
            part = weight[taps:, :channels]
        return acc[tile_at(t), side * channels : (side + 1) * channels] + dot(
            around(base + 2 + side, t), part
        )

    def repeat(count, body):
        def step(t, carry):
            body(t)
            return carry

        lax.fori_loop(0, count, step, 0)

    cells = tile // depth
    cube = (cells, depth, across)

    def spread_tile(t):
        lane = lax.broadcasted_iota(jnp.int32, cube, 2)
        cell = lax.broadcasted_iota(jnp.int32, cube, 0) + t * cells
        for side in range(2):
            field = jnp.broadcast_to(prior[side][None], cube)
            field = jnp.sum(jnp.where(lane == cell, field, 0.0), axis=2, keepdims=True)
            field = jnp.broadcast_to(field, (cells, depth, channels))
            spread[side, tile_at(t), :] = field.reshape(tile, channels)

    for copy in vox_loads + loads[:4]:
        copy.wait()

    @functools.partial(repeat, tiles + 1)
    def _(t):
        @pl.when(t < tiles)
        def _():
            for side in range(2):
                stack_tile(side, vox.at[side], t)

        @pl.when(t == tiles)
        def _():
            for side in range(2):
                stack_end(side, vox.at[side])

        @pl.when(t >= 1)
        def _():
            spread_tile(t - 1)
            inner(0, w_first, t - 1)

    for copy in loads[4:]:
        copy.wait()

    @functools.partial(repeat, tiles + 2)
    def _(t):
        @pl.when(t < tiles)
        def _():
            face_tile(0, face_vox, vox_copy, t)

        @pl.when(t == tiles)
        def _():
            for side in range(2):
                stack_end(2 + side, face_vox.at[side])

        @pl.when(jnp.logical_and(t >= 1, t <= tiles))
        def _():
            u = t - 1
            for side, has in ((0, has_left), (1, has_right)):
                value = activate(outer(0, w_first, side, u)).astype(BF16)
                first[side, tile_at(u, PAD), :] = value

                @pl.when(has)
                def _():
                    first_copy(side, u).start()

            for side in range(2):
                stack_tile(4 + side, first.at[side], u)

        @pl.when(t == tiles)
        def _():
            for side in range(2):
                stack_end(4 + side, first.at[side])

        @pl.when(t >= 2)
        def _():
            inner(4, w_second, t - 2)

    running[:, 0] = jnp.full((2, depth, channels), -jnp.inf, F32)
    running[:, 1:] = jnp.zeros((2, 2, depth, channels), F32)

    def local_part(t):
        logits, features = [], []
        for side in range(2):
            value = outer(4, w_second, side, t)
            value += vox[side, tile_at(t, PAD), :].astype(F32)
            value = value.astype(BF16)
            feature[side, tile_at(t), :] = value
            both = dot(value, w_score[...])
            field = spread[side, tile_at(t), :]
            value = value.astype(F32)
            logits.append(both[:, :channels] + field)
            features.append(value)
            logit_y = (both[:, channels:] + field).reshape(cells, depth, channels)
            value = value.reshape(cells, depth, channels)
            old, norm, total = running[side, 0], running[side, 1], running[side, 2]
            peak = jnp.maximum(jnp.max(logit_y, axis=0), old)
            weight = jnp.exp(logit_y - peak[None])
            keep = jnp.exp(old - peak)
            running[side, 0] = peak
            running[side, 1] = norm * keep + jnp.sum(weight, 0)
            running[side, 2] = total * keep + jnp.sum(weight * value, 0)
        peak = jnp.maximum(logits[0], logits[1]).astype(BF16)
        weights = [jnp.exp(logit - peak.astype(F32)) for logit in logits]
        stats[0, tile_at(t), :] = peak
        stats[1, tile_at(t), :] = (weights[0] + weights[1]).astype(BF16)
        stats[2, tile_at(t), :] = (weights[0] * features[0] + weights[1] * features[1]).astype(BF16)

    def rows_at(start, rows):
        return pl.ds(pl.multiple_of(start, 16), rows)

    def start_of(g, k):
        start = g * tile
        for digit, (_, _, rows, shares) in zip(digits[:k], stages):
            if shares:
                start = start + digit * rows
        return start

    def reduce_copies(g, k):
        distance, radix, rows, shares = stages[k]
        copies = []
        for hop in range(1, radix):
            partner, theirs = partners[k][hop]
            give = start_of(g, k)
            if shares:
                give = give + theirs * rows
            copies.append(
                pltpu.make_async_remote_copy(
                    src_ref=stats.at[:, rows_at(give, rows), :],
                    dst_ref=halves[k].at[g, hop - 1],
                    send_sem=rs_send.at[g, slots[k] + hop - 1],
                    recv_sem=rs_recv.at[g, slots[k] + hop - 1],
                    device_id={"gx": partner},
                    device_id_type=MESH,
                )
            )
        return copies

    def reduce_end(g, k):
        distance, radix, rows, shares = stages[k]
        for copy in reduce_copies(g, k):
            copy.wait_recv()
            if not shares:
                copy.wait_send()
        start = start_of(g, k + 1)
        at = rows_at(start, rows)
        held = [stats[:, at, :].astype(F32)]
        held += [halves[k][g, hop].astype(F32) for hop in range(radix - 1)]
        peak = functools.reduce(jnp.maximum, [each[0] for each in held])
        scales = [jnp.exp(each[0] - peak) for each in held]
        norm = sum(each[1] * scale for each, scale in zip(held, scales))
        total = sum(each[2] * scale for each, scale in zip(held, scales))
        if k + 1 < len(stages):
            for i, value in enumerate((peak, norm, total)):
                stats[i, at, :] = value.astype(BF16)
        else:
            pooled[rows_at(PAD + start, rows), :] = (total / norm).astype(BF16)

    def gather_copy(g, slot, start, rows, partner):
        part = pooled.at[rows_at(PAD + start, rows), :]
        return pltpu.make_async_remote_copy(
            src_ref=part,
            dst_ref=part,
            send_sem=ag_send.at[g, slot],
            recv_sem=ag_recv.at[g, slot],
            device_id={"gx": partner},
            device_id_type=MESH,
        )

    def far_copies(g):
        start, rows = start_of(g, len(stages)), stages[-1][2]
        return [gather_copy(g, i, start, rows, partner) for i, partner in enumerate(far)]

    def near_copies(g):
        rows = stages[0][2]
        return [gather_copy(g, len(far), start_of(g, 1), rows, partners[0][1][0])]

    def strip_copy(side):
        return pltpu.make_async_remote_copy(
            src_ref=strip.at[1 + side],
            dst_ref=strip.at[3 - 3 * side],
            send_sem=strip_send.at[side],
            recv_sem=strip_recv.at[1 - side],
            device_id={"gx": (left, right)[side]},
            device_id_type=MESH,
        )

    def strip_start():
        for side, has in ((0, has_left), (1, has_right)):
            strip[1 + side] = (running[side, 2] / running[side, 1]).astype(BF16).astype(F32)

            @pl.when(has)
            def _():
                strip_copy(side).start()

    def strip_plane():
        for side, has in ((0, has_left), (1, has_right)):

            @pl.when(has)
            def _():
                strip_copy(1 - side).wait_recv()

        moved = shifted(strip[...])
        stacked = [
            jnp.concatenate([part[x + i] for i in range(3) for part in moved], axis=1)
            for x in range(2)
        ]
        plane = dot(jnp.concatenate(stacked, axis=0).astype(BF16), w_xz[...])
        plane_xz[...] = plane.astype(BF16).astype(F32)

    def finish(t):
        plane_yz = dot(around(8, t), w_yz[...])
        plane_yz = plane_yz.astype(BF16).astype(F32).reshape(cells, depth, channels)
        for side in range(2):
            mixing = plane_yz + plane_xz[side * depth : (side + 1) * depth, :][None]
            joined = feature[side, tile_at(t), :].astype(F32) * mixing.reshape(tile, channels)
            squares = dot((joined * joined).astype(BF16), jnp.ones((channels, channels), BF16))
            scale = lax.rsqrt(squares * (1.0 / channels) + 1e-06)
            normed = (joined * scale * norm_gain[...]).astype(BF16)
            hidden = activate(dot(normed, w_in[...])).astype(BF16)
            out[side, tile_at(t), :] = (joined + dot(hidden, w_out[...])).astype(BF16)

    last = len(stages)

    @functools.partial(repeat, tiles + last + 4)
    def _(slot):
        @pl.when(slot < tiles)
        def _():
            face_tile(4, face_first, first_copy, slot)

        @pl.when(slot == tiles)
        def _():
            for side in range(2):
                stack_end(6 + side, face_first.at[side])

        @pl.when(jnp.logical_and(slot >= 1, slot <= tiles))
        def _():
            local_part(slot - 1)

        def at_step(step, body):
            g = slot - 1 - step

            @pl.when(jnp.logical_and(g >= 0, g < tiles))
            def _():
                body(g)

        def start_all(copies):
            for copy in copies:
                copy.start()

        def end_all(copies):
            for copy in copies:
                copy.wait_recv()

        def advance(k, g):
            if k > 0:
                reduce_end(g, k - 1)
            start_all(reduce_copies(g, k) if k < last else far_copies(g))

        def gather_near(g):
            end_all(far_copies(g))
            start_all(near_copies(g))

        def gather_end(g):
            end_all(near_copies(g))
            stack_tile(8, pooled, g)

            @pl.when(g == tiles - 1)
            def _():
                stack_end(8, pooled)

        for k in range(last + 1):
            at_step(k, functools.partial(advance, k))
        at_step(last + 1, gather_near)
        at_step(last + 2, gather_end)

        @pl.when(slot == tiles)
        def _():
            strip_start()

        @pl.when(slot == tiles + 1)
        def _():
            strip_plane()

        at_step(last + 3, finish)

    @functools.partial(repeat, tiles)
    def _(g):
        for k, (_, _, _, shares) in enumerate(stages):
            for copy in reduce_copies(g, k) if shares else []:
                copy.wait_send()
        for copy in far_copies(g) + near_copies(g):
            copy.wait_send()

    sent(vox_copy)
    sent(first_copy)
    for side, has in ((0, has_left), (1, has_right)):

        @pl.when(has)
        def _():
            strip_copy(side).wait_send()


def on_device(
    n,
    voxels,
    prior,
    conv_first,
    conv_second,
    score_x,
    score_y,
    plane_yz_w,
    plane_xz_w,
    norm_gain,
    mlp_in,
    mlp_out,
):
    rows, across, depth, channels = voxels.shape
    assert rows == 2 and depth == 8 and n & (n - 1) == 0
    length = across * depth
    hidden = mlp_in.shape[1]
    tile = min(256, length)
    tiles = length // tile
    stages = stages_of(tile, n)
    exchanges = sum(stage[1] - 1 for stage in stages)
    padded = length + 2 * PAD
    taps = conv_first.shape[0] // 3 * channels
    hbm = pl.BlockSpec(memory_space=pl.ANY)
    vmem = pl.BlockSpec(memory_space=pltpu.VMEM)
    result = pl.pallas_call(
        functools.partial(kernel, n, tile, stages),
        out_shape=jax.ShapeDtypeStruct((rows, length, channels), BF16),
        in_specs=[hbm, vmem, hbm, hbm, hbm, hbm, hbm, hbm, vmem, hbm, hbm],
        out_specs=vmem,
        scratch_shapes=[
            pltpu.VMEM((2 * taps, 2 * channels), BF16),
            pltpu.VMEM((2 * taps, 2 * channels), BF16),
            pltpu.VMEM((channels, 2 * channels), BF16),
            pltpu.VMEM((taps, channels), BF16),
            pltpu.VMEM((taps, channels), BF16),
            pltpu.VMEM((channels, hidden), BF16),
            pltpu.VMEM((hidden, channels), BF16),
            pltpu.VMEM((2, padded, channels), BF16),
            pltpu.VMEM((2, padded, channels), BF16),
            pltpu.VMEM((2, padded, channels), BF16),
            pltpu.VMEM((2, padded, channels), BF16),
            pltpu.VMEM((length, 2 * channels), F32),
            pltpu.VMEM((2, length, channels), BF16),
            pltpu.VMEM((3, length, channels), BF16),
            pltpu.VMEM((padded, channels), BF16),
            pltpu.VMEM((4, depth, channels), F32),
            pltpu.VMEM((2, 3, depth, channels), F32),
            pltpu.VMEM((2 * depth, channels), F32),
            pltpu.VMEM((2, length, channels), F32),
            pltpu.VMEM((9, padded, 3 * channels), BF16),
            pltpu.VMEM((9, padded, 3 * channels), BF16),
            [
                pltpu.VMEM((tiles, radix - 1, 3, share, channels), BF16)
                for _, radix, share, _ in stages
            ],
            pltpu.SemaphoreType.DMA((14,)),
            pltpu.SemaphoreType.DMA((2,)),
            pltpu.SemaphoreType.DMA((2, 2, tiles)),
            pltpu.SemaphoreType.DMA((2, 2, tiles)),
            pltpu.SemaphoreType.DMA((2,)),
            pltpu.SemaphoreType.DMA((2,)),
            pltpu.SemaphoreType.DMA((tiles, exchanges)),
            pltpu.SemaphoreType.DMA((tiles, exchanges)),
            pltpu.SemaphoreType.DMA((tiles, far_radix(stages))),
            pltpu.SemaphoreType.DMA((tiles, far_radix(stages))),
        ],
        compiler_params=pltpu.CompilerParams(
            collective_id=0, has_side_effects=True, vmem_limit_bytes=62 * 1024 * 1024
        ),
    )(
        voxels.reshape(rows, length, channels),
        prior.transpose(0, 2, 1),
        conv_first.reshape(3, taps, channels),
        conv_second.reshape(3, taps, channels),
        score_x,
        score_y,
        plane_yz_w.reshape(taps, channels),
        plane_xz_w.reshape(taps, channels),
        norm_gain.reshape(1, channels),
        mlp_in,
        mlp_out,
    )
    return result.reshape(voxels.shape)


def solution(mesh):
    split = P(("scene", "gx"), None, None, None)
    return jax.shard_map(
        functools.partial(on_device, mesh.shape["gx"]),
        mesh=mesh,
        in_specs=(split, P(("scene", "gx"), None, None)) + (P(),) * 9,
        out_specs=split,
        check_vma=False,
    )
```

```python
import functools

import jax
import jax.numpy as jnp
from jax import lax
from jax.experimental import pallas as pl
from jax.experimental.pallas import tpu as pltpu
from jax.sharding import PartitionSpec as P

MESH = pl.DeviceIdType.MESH
PAD = 16
F32 = jnp.float32
BF16 = jnp.bfloat16


def activate(values):
    return jax.nn.gelu(values, approximate=True)


def stages_of(rows, devices):
    count = devices.bit_length() - 1
    bits = [[i] for i in range(min(2, count))]
    bits += [list(range(i, min(i + 2, count))) for i in range(2, count, 2)]
    stages = []
    for group in bits:
        radix = 1 << len(group)
        shares = rows % (16 * radix) == 0
        rows = rows // radix if shares else rows
        stages.append((1 << group[0], radix, rows, shares))
    return stages


def far_radix(stages):
    total = 1
    for distance, radix, _, shares in stages:
        if shares and distance > 1:
            total *= radix
    return total


def shifted(values):
    depth = values.shape[1]
    at_z = lax.broadcasted_iota(jnp.int32, (1,) + values.shape[1:], 1)
    below = jnp.where(at_z == 0, 0.0, pltpu.roll(values, 1, 1))
    above = jnp.where(at_z == depth - 1, 0.0, pltpu.roll(values, depth - 1, 1))
    return below, values, above


def stack(source, even, odd, start, rows, depth):
    channels = source.shape[1]
    window = source[pl.ds(pl.multiple_of(start - PAD, 16), rows + PAD), :].astype(F32)
    parts = shifted(window.reshape(-1, depth, channels))
    at = pl.ds(pl.multiple_of(start, 16), rows)
    for i, part in enumerate(parts):
        part = part.reshape(rows + PAD, channels)
        columns = slice(i * channels, (i + 1) * channels)
        even[at, columns] = part[PAD:].astype(BF16)
        odd[at, columns] = part[PAD - depth : rows + PAD - depth].astype(BF16)


def neighbourhood(even, odd, start, tile):
    first = pl.ds(pl.multiple_of(start, 16), tile)
    after = pl.ds(pl.multiple_of(start + PAD, 16), tile)
    return jnp.concatenate([odd[first, :], even[first, :], odd[after, :]], axis=1)


def dot(a, b):
    return jnp.dot(a, b, preferred_element_type=F32)


def kernel(
    n,
    tile,
    stages,
    voxels,
    prior,
    conv_first,
    conv_second,
    score_x,
    score_y,
    plane_yz_w,
    plane_xz_w,
    norm_gain,
    mlp_in,
    mlp_out,
    out,
    w_first,
    w_second,
    w_score,
    w_yz,
    w_xz,
    w_in,
    w_out,
    vox,
    face_vox,
    first,
    face_first,
    acc,
    feature,
    stats,
    pooled,
    strip,
    running,
    plane_xz,
    spread,
    even,
    odd,
    halves,
    load_sem,
    vox_sem,
    face_send,
    face_recv,
    strip_send,
    strip_recv,
    rs_send,
    rs_recv,
    ag_send,
    ag_recv,
):
    me = lax.axis_index("gx")
    length, channels = voxels.shape[1], voxels.shape[2]
    depth = prior.shape[1]
    tiles = length // tile
    has_left, has_right = me > 0, me < n - 1
    left, right = me - 1, me + 1
    across = length // depth

    def across_bits(distance, hop):
        other, weight = me, 1
        while weight <= hop:
            bit = (me // (distance * weight)) % 2
            if hop & weight:
                other = other + (1 - 2 * bit) * distance * weight
            weight *= 2
        return other

    digits = [(me // distance) % radix for distance, radix, _, _ in stages]
    partners = []
    for distance, radix, _, _ in stages:
        found = {}
        for hop in range(1, radix):
            other = across_bits(distance, hop)
            found[hop] = (other, (other // distance) % radix)
        partners.append(found)
    slots = [sum(stage[1] - 1 for stage in stages[:k]) for k in range(len(stages))]
    far = [across_bits(2, hop) for hop in range(1, far_radix(stages))]

    taps = conv_first.shape[1]
    loads = []
    for source, target in ((conv_first, w_first), (conv_second, w_second)):
        for layer in range(2):
            for result in range(2):
                block = (pl.ds(layer * taps, taps), pl.ds(result * channels, channels))
                loads.append((source.at[1 + layer - result], target.at[block]))
    loads += [
        (score_x, w_score.at[:, pl.ds(0, channels)]),
        (score_y, w_score.at[:, pl.ds(channels, channels)]),
        (plane_yz_w, w_yz),
        (plane_xz_w, w_xz),
        (mlp_in, w_in),
        (mlp_out, w_out),
    ]
    vox_loads = [
        pltpu.make_async_copy(
            voxels.at[row], vox.at[row, pl.ds(PAD, length), :], vox_sem.at[row]
        )
        for row in range(2)
    ]
    loads = [
        pltpu.make_async_copy(source, target, load_sem.at[i])
        for i, (source, target) in enumerate(loads)
    ]
    for copy in vox_loads + loads:
        copy.start()

    barrier = pltpu.get_barrier_semaphore()
    greeted = far + [
        partner
        for stage, found in zip(stages, partners)
        for partner, _ in found.values()
        if stage[0] == 1 or not stage[3]
    ]
    for partner in greeted:
        pl.semaphore_signal(barrier, inc=1, device_id={"gx": partner}, device_id_type=MESH)

    @pl.when(has_left)
    def _():
        pl.semaphore_signal(barrier, inc=1, device_id={"gx": left}, device_id_type=MESH)

    @pl.when(has_right)
    def _():
        pl.semaphore_signal(barrier, inc=1, device_id={"gx": right}, device_id_type=MESH)

    edge = jnp.zeros((2, PAD, channels), BF16)
    for padded in (vox, face_vox, first, face_first):
        padded[:, 0:PAD, :] = edge
        padded[:, PAD + length :, :] = edge
    pooled[0:PAD, :] = edge[0]
    pooled[PAD + length :, :] = edge[0]

    for side, has in ((0, has_left), (1, has_right)):

        @pl.when(jnp.logical_not(has))
        def _():
            blank = jnp.zeros((length, channels), BF16)
            face_vox[side, pl.ds(PAD, length), :] = blank
            face_first[side, pl.ds(PAD, length), :] = blank
            strip[3 * side] = jnp.zeros(strip.shape[1:], F32)

    pl.semaphore_wait(barrier, len(greeted) + jnp.where(has_left, 1, 0) + jnp.where(has_right, 1, 0))

    def face_copy(which, source, target, side, t, to):
        return pltpu.make_async_remote_copy(
            src_ref=source,
            dst_ref=target.at[1 - side, pl.ds(pl.multiple_of(PAD + t * tile, 16), tile), :],
            send_sem=face_send.at[which, side, t],
            recv_sem=face_recv.at[which, 1 - side, t],
            device_id={"gx": to},
            device_id_type=MESH,
        )

    def vox_copy(side, t):
        source = voxels.at[side, pl.ds(pl.multiple_of(t * tile, 16), tile), :]
        return face_copy(0, source, face_vox, side, t, (left, right)[side])

    def first_copy(side, t):
        source = first.at[side, pl.ds(pl.multiple_of(PAD + t * tile, 16), tile), :]
        return face_copy(1, source, face_first, side, t, (left, right)[side])

    def arrive(make, side, t, has):
        @pl.when(has)
        def _():
            make(1 - side, t).wait_recv()

    def sent(make):
        for side, has in ((0, has_left), (1, has_right)):

            @pl.when(has)
            def _():
                for t in range(tiles):
                    make(side, t).wait_send()

    for t in range(tiles):
        for side, has in ((0, has_left), (1, has_right)):

            @pl.when(has)
            def _():
                vox_copy(side, t).start()

    def stack_tile(layer, source, t):
        stack(source, even.at[layer], odd.at[layer], PAD + t * tile, tile, depth)

    def stack_end(layer, source):
        stack(source, even.at[layer], odd.at[layer], PAD + length, PAD, depth)

    def around(layer, t):
        return neighbourhood(even.at[layer], odd.at[layer], PAD + t * tile, tile)

    def tile_at(t, offset=0):
        return pl.ds(pl.multiple_of(offset + t * tile, 16), tile)

    def inner(base, weight, t):
        both = jnp.concatenate([around(base, t), around(base + 1, t)], axis=1)
        acc[tile_at(t), :] = dot(both, weight[...])

    def face_tile(base, face, make, t):
        for side, has in ((0, has_left), (1, has_right)):
            arrive(make, side, t, has)
            stack_tile(base + 2 + side, face.at[side], t)

    def outer(base, weight, side, t):
        if side == 0:
            part = weight[:taps, channels:]
        else:
            part = weight[taps:, :channels]
        return acc[tile_at(t), side * channels : (side + 1) * channels] + dot(
            around(base + 2 + side, t), part
        )

    def repeat(count, body):
        def step(t, carry):
            body(t)
            return carry

        lax.fori_loop(0, count, step, 0)

    cells = tile // depth
    cube = (cells, depth, across)

    def spread_tile(t):
        lane = lax.broadcasted_iota(jnp.int32, cube, 2)
        cell = lax.broadcasted_iota(jnp.int32, cube, 0) + t * cells
        for side in range(2):
            field = jnp.broadcast_to(prior[side][None], cube)
            field = jnp.sum(jnp.where(lane == cell, field, 0.0), axis=2, keepdims=True)
            field = jnp.broadcast_to(field, (cells, depth, channels))
            spread[side, tile_at(t), :] = field.reshape(tile, channels)

    for copy in vox_loads + loads[:4]:
        copy.wait()

    @functools.partial(repeat, tiles + 1)
    def _(t):
        @pl.when(t < tiles)
        def _():
            for side in range(2):
                stack_tile(side, vox.at[side], t)

        @pl.when(t == tiles)
        def _():
            for side in range(2):
                stack_end(side, vox.at[side])

        @pl.when(t >= 1)
        def _():
            spread_tile(t - 1)
            inner(0, w_first, t - 1)

    for copy in loads[4:]:
        copy.wait()

    @functools.partial(repeat, tiles + 2)
    def _(t):
        @pl.when(t < tiles)
        def _():
            face_tile(0, face_vox, vox_copy, t)

        @pl.when(t == tiles)
        def _():
            for side in range(2):
                stack_end(2 + side, face_vox.at[side])

        @pl.when(jnp.logical_and(t >= 1, t <= tiles))
        def _():
            u = t - 1
            for side, has in ((0, has_left), (1, has_right)):
                value = activate(outer(0, w_first, side, u)).astype(BF16)
                first[side, tile_at(u, PAD), :] = value

                @pl.when(has)
                def _():
                    first_copy(side, u).start()

            for side in range(2):
                stack_tile(4 + side, first.at[side], u)

        @pl.when(t == tiles)
        def _():
            for side in range(2):
                stack_end(4 + side, first.at[side])

        @pl.when(t >= 2)
        def _():
            inner(4, w_second, t - 2)

    running[:, 0] = jnp.full((2, depth, channels), -jnp.inf, F32)
    running[:, 1:] = jnp.zeros((2, 2, depth, channels), F32)

    def local_part(t):
        logits, features = [], []
        for side in range(2):
            value = outer(4, w_second, side, t)
            value += vox[side, tile_at(t, PAD), :].astype(F32)
            value = value.astype(BF16)
            feature[side, tile_at(t), :] = value
            both = dot(value, w_score[...])
            field = spread[side, tile_at(t), :]
            value = value.astype(F32)
            logits.append(both[:, :channels] + field)
            features.append(value)
            logit_y = (both[:, channels:] + field).reshape(cells, depth, channels)
            value = value.reshape(cells, depth, channels)
            old, norm, total = running[side, 0], running[side, 1], running[side, 2]
            peak = jnp.maximum(jnp.max(logit_y, axis=0), old)
            weight = jnp.exp(logit_y - peak[None])
            keep = jnp.exp(old - peak)
            running[side, 0] = peak
            running[side, 1] = norm * keep + jnp.sum(weight, 0)
            running[side, 2] = total * keep + jnp.sum(weight * value, 0)
        peak = jnp.maximum(logits[0], logits[1]).astype(BF16)
        weights = [jnp.exp(logit - peak.astype(F32)) for logit in logits]
        stats[0, tile_at(t), :] = peak
        stats[1, tile_at(t), :] = (weights[0] + weights[1]).astype(BF16)
        stats[2, tile_at(t), :] = (weights[0] * features[0] + weights[1] * features[1]).astype(BF16)

    def rows_at(start, rows):
        return pl.ds(pl.multiple_of(start, 16), rows)

    def start_of(g, k):
        start = g * tile
        for digit, (_, _, rows, shares) in zip(digits[:k], stages):
            if shares:
                start = start + digit * rows
        return start

    def reduce_copies(g, k):
        distance, radix, rows, shares = stages[k]
        copies = []
        for hop in range(1, radix):
            partner, theirs = partners[k][hop]
            give = start_of(g, k)
            if shares:
                give = give + theirs * rows
            copies.append(
                pltpu.make_async_remote_copy(
                    src_ref=stats.at[:, rows_at(give, rows), :],
                    dst_ref=halves[k].at[g, hop - 1],
                    send_sem=rs_send.at[g, slots[k] + hop - 1],
                    recv_sem=rs_recv.at[g, slots[k] + hop - 1],
                    device_id={"gx": partner},
                    device_id_type=MESH,
                )
            )
        return copies

    def reduce_end(g, k):
        distance, radix, rows, shares = stages[k]
        for copy in reduce_copies(g, k):
            copy.wait_recv()
            if not shares:
                copy.wait_send()
        start = start_of(g, k + 1)
        at = rows_at(start, rows)
        held = [stats[:, at, :].astype(F32)]
        held += [halves[k][g, hop].astype(F32) for hop in range(radix - 1)]
        peak = functools.reduce(jnp.maximum, [each[0] for each in held])
        scales = [jnp.exp(each[0] - peak) for each in held]
        norm = sum(each[1] * scale for each, scale in zip(held, scales))
        total = sum(each[2] * scale for each, scale in zip(held, scales))
        if k + 1 < len(stages):
            for i, value in enumerate((peak, norm, total)):
                stats[i, at, :] = value.astype(BF16)
        else:
            pooled[rows_at(PAD + start, rows), :] = (total / norm).astype(BF16)

    def gather_copy(g, slot, start, rows, partner):
        part = pooled.at[rows_at(PAD + start, rows), :]
        return pltpu.make_async_remote_copy(
            src_ref=part,
            dst_ref=part,
            send_sem=ag_send.at[g, slot],
            recv_sem=ag_recv.at[g, slot],
            device_id={"gx": partner},
            device_id_type=MESH,
        )

    def far_copies(g):
        start, rows = start_of(g, len(stages)), stages[-1][2]
        return [gather_copy(g, i, start, rows, partner) for i, partner in enumerate(far)]

    def near_copies(g):
        rows = stages[0][2]
        return [gather_copy(g, len(far), start_of(g, 1), rows, partners[0][1][0])]

    def strip_copy(side):
        return pltpu.make_async_remote_copy(
            src_ref=strip.at[1 + side],
            dst_ref=strip.at[3 - 3 * side],
            send_sem=strip_send.at[side],
            recv_sem=strip_recv.at[1 - side],
            device_id={"gx": (left, right)[side]},
            device_id_type=MESH,
        )

    def strip_start():
        for side, has in ((0, has_left), (1, has_right)):
            strip[1 + side] = (running[side, 2] / running[side, 1]).astype(BF16).astype(F32)

            @pl.when(has)
            def _():
                strip_copy(side).start()

    def strip_plane():
        for side, has in ((0, has_left), (1, has_right)):

            @pl.when(has)
            def _():
                strip_copy(1 - side).wait_recv()

        moved = shifted(strip[...])
        stacked = [
            jnp.concatenate([part[x + i] for i in range(3) for part in moved], axis=1)
            for x in range(2)
        ]
        plane = dot(jnp.concatenate(stacked, axis=0).astype(BF16), w_xz[...])
        plane_xz[...] = plane.astype(BF16).astype(F32)

    def finish(t):
        plane_yz = dot(around(8, t), w_yz[...])
        plane_yz = plane_yz.astype(BF16).astype(F32).reshape(cells, depth, channels)
        for side in range(2):
            mixing = plane_yz + plane_xz[side * depth : (side + 1) * depth, :][None]
            joined = feature[side, tile_at(t), :].astype(F32) * mixing.reshape(tile, channels)
            squares = dot((joined * joined).astype(BF16), jnp.ones((channels, channels), BF16))
            scale = lax.rsqrt(squares * (1.0 / channels) + 1e-06)
            normed = (joined * scale * norm_gain[...]).astype(BF16)
            hidden = activate(dot(normed, w_in[...])).astype(BF16)
            out[side, tile_at(t), :] = (joined + dot(hidden, w_out[...])).astype(BF16)

    last = len(stages)

    @functools.partial(repeat, tiles + last + 4)
    def _(slot):
        @pl.when(slot < tiles)
        def _():
            face_tile(4, face_first, first_copy, slot)

        @pl.when(slot == tiles)
        def _():
            for side in range(2):
                stack_end(6 + side, face_first.at[side])

        @pl.when(jnp.logical_and(slot >= 1, slot <= tiles))
        def _():
            local_part(slot - 1)

        def at_step(step, body):
            g = slot - 1 - step

            @pl.when(jnp.logical_and(g >= 0, g < tiles))
            def _():
                body(g)

        def start_all(copies):
            for copy in copies:
                copy.start()

        def end_all(copies):
            for copy in copies:
                copy.wait_recv()

        def advance(k, g):
            if k > 0:
                reduce_end(g, k - 1)
            start_all(reduce_copies(g, k) if k < last else far_copies(g))

        def gather_near(g):
            end_all(far_copies(g))
            start_all(near_copies(g))

        def gather_end(g):
            end_all(near_copies(g))
            stack_tile(8, pooled, g)

            @pl.when(g == tiles - 1)
            def _():
                stack_end(8, pooled)

        for k in range(last + 1):
            at_step(k, functools.partial(advance, k))
        at_step(last + 1, gather_near)
        at_step(last + 2, gather_end)

        @pl.when(slot == tiles)
        def _():
            strip_start()

        @pl.when(slot == tiles + 1)
        def _():
            strip_plane()

        at_step(last + 3, finish)

    @functools.partial(repeat, tiles)
    def _(g):
        for k, (_, _, _, shares) in enumerate(stages):
            for copy in reduce_copies(g, k) if shares else []:
                copy.wait_send()
        for copy in far_copies(g) + near_copies(g):
            copy.wait_send()

    sent(vox_copy)
    sent(first_copy)
    for side, has in ((0, has_left), (1, has_right)):

        @pl.when(has)
        def _():
            strip_copy(side).wait_send()


def on_device(
    n,
    voxels,
    prior,
    conv_first,
    conv_second,
    score_x,
    score_y,
    plane_yz_w,
    plane_xz_w,
    norm_gain,
    mlp_in,
    mlp_out,
):
    rows, across, depth, channels = voxels.shape
    assert rows == 2 and depth == 8 and n & (n - 1) == 0
    length = across * depth
    hidden = mlp_in.shape[1]
    tile = min(512, length)
    tiles = length // tile
    stages = stages_of(tile, n)
    exchanges = sum(stage[1] - 1 for stage in stages)
    padded = length + 2 * PAD
    taps = conv_first.shape[0] // 3 * channels
    hbm = pl.BlockSpec(memory_space=pl.ANY)
    vmem = pl.BlockSpec(memory_space=pltpu.VMEM)
    result = pl.pallas_call(
        functools.partial(kernel, n, tile, stages),
        out_shape=jax.ShapeDtypeStruct((rows, length, channels), BF16),
        in_specs=[hbm, vmem, hbm, hbm, hbm, hbm, hbm, hbm, vmem, hbm, hbm],
        out_specs=vmem,
        scratch_shapes=[
            pltpu.VMEM((2 * taps, 2 * channels), BF16),
            pltpu.VMEM((2 * taps, 2 * channels), BF16),
            pltpu.VMEM((channels, 2 * channels), BF16),
            pltpu.VMEM((taps, channels), BF16),
            pltpu.VMEM((taps, channels), BF16),
            pltpu.VMEM((channels, hidden), BF16),
            pltpu.VMEM((hidden, channels), BF16),
            pltpu.VMEM((2, padded, channels), BF16),
            pltpu.VMEM((2, padded, channels), BF16),
            pltpu.VMEM((2, padded, channels), BF16),
            pltpu.VMEM((2, padded, channels), BF16),
            pltpu.VMEM((length, 2 * channels), F32),
            pltpu.VMEM((2, length, channels), BF16),
            pltpu.VMEM((3, length, channels), BF16),
            pltpu.VMEM((padded, channels), BF16),
            pltpu.VMEM((4, depth, channels), F32),
            pltpu.VMEM((2, 3, depth, channels), F32),
            pltpu.VMEM((2 * depth, channels), F32),
            pltpu.VMEM((2, length, channels), F32),
            pltpu.VMEM((9, padded, 3 * channels), BF16),
            pltpu.VMEM((9, padded, 3 * channels), BF16),
            [
                pltpu.VMEM((tiles, radix - 1, 3, share, channels), BF16)
                for _, radix, share, _ in stages
            ],
            pltpu.SemaphoreType.DMA((14,)),
            pltpu.SemaphoreType.DMA((2,)),
            pltpu.SemaphoreType.DMA((2, 2, tiles)),
            pltpu.SemaphoreType.DMA((2, 2, tiles)),
            pltpu.SemaphoreType.DMA((2,)),
            pltpu.SemaphoreType.DMA((2,)),
            pltpu.SemaphoreType.DMA((tiles, exchanges)),
            pltpu.SemaphoreType.DMA((tiles, exchanges)),
            pltpu.SemaphoreType.DMA((tiles, far_radix(stages))),
            pltpu.SemaphoreType.DMA((tiles, far_radix(stages))),
        ],
        compiler_params=pltpu.CompilerParams(
            collective_id=0, has_side_effects=True, vmem_limit_bytes=62 * 1024 * 1024
        ),
    )(
        voxels.reshape(rows, length, channels),
        prior.transpose(0, 2, 1),
        conv_first.reshape(3, taps, channels),
        conv_second.reshape(3, taps, channels),
        score_x,
        score_y,
        plane_yz_w.reshape(taps, channels),
        plane_xz_w.reshape(taps, channels),
        norm_gain.reshape(1, channels),
        mlp_in,
        mlp_out,
    )
    return result.reshape(voxels.shape)


def solution(mesh):
    split = P(("scene", "gx"), None, None, None)
    return jax.shard_map(
        functools.partial(on_device, mesh.shape["gx"]),
        mesh=mesh,
        in_specs=(split, P(("scene", "gx"), None, None)) + (P(),) * 9,
        out_specs=split,
        check_vma=False,
    )
```

```python
import functools

import jax
import jax.numpy as jnp
from jax import lax
from jax.experimental import pallas as pl
from jax.experimental.pallas import tpu as pltpu
from jax.sharding import PartitionSpec as P

MESH = pl.DeviceIdType.MESH
PAD = 16
F32 = jnp.float32
BF16 = jnp.bfloat16


def activate(values):
    return jax.nn.gelu(values, approximate=True)


def stages_of(rows, devices):
    count = devices.bit_length() - 1
    bits = [[i] for i in range(count)]
    bits[1:4] = bits[2:4] + bits[1:2]
    stages = []
    for group in bits:
        radix = 1 << len(group)
        shares = rows % (16 * radix) == 0
        rows = rows // radix if shares else rows
        stages.append((1 << group[0], radix, rows, shares))
    return stages


def far_radix(stages):
    total = 1
    for distance, radix, _, shares in stages:
        if shares and distance > 1:
            total *= radix
    return total


def shifted(values):
    depth = values.shape[1]
    at_z = lax.broadcasted_iota(jnp.int32, (1,) + values.shape[1:], 1)
    below = jnp.where(at_z == 0, 0.0, pltpu.roll(values, 1, 1))
    above = jnp.where(at_z == depth - 1, 0.0, pltpu.roll(values, depth - 1, 1))
    return below, values, above


def stack(source, even, odd, start, rows, depth):
    channels = source.shape[1]
    window = source[pl.ds(pl.multiple_of(start - PAD, 16), rows + PAD), :].astype(F32)
    parts = shifted(window.reshape(-1, depth, channels))
    at = pl.ds(pl.multiple_of(start, 16), rows)
    for i, part in enumerate(parts):
        part = part.reshape(rows + PAD, channels)
        columns = slice(i * channels, (i + 1) * channels)
        even[at, columns] = part[PAD:].astype(BF16)
        odd[at, columns] = part[PAD - depth : rows + PAD - depth].astype(BF16)


def neighbourhood(even, odd, start, tile):
    first = pl.ds(pl.multiple_of(start, 16), tile)
    after = pl.ds(pl.multiple_of(start + PAD, 16), tile)
    return jnp.concatenate([odd[first, :], even[first, :], odd[after, :]], axis=1)


def dot(a, b):
    return jnp.dot(a, b, preferred_element_type=F32)


def kernel(
    n,
    tile,
    stages,
    voxels,
    prior,
    conv_first,
    conv_second,
    score_x,
    score_y,
    plane_yz_w,
    plane_xz_w,
    norm_gain,
    mlp_in,
    mlp_out,
    out,
    w_first,
    w_second,
    w_score,
    w_yz,
    w_xz,
    w_in,
    w_out,
    vox,
    face_vox,
    first,
    face_first,
    acc,
    feature,
    stats,
    pooled,
    strip,
    running,
    plane_xz,
    spread,
    even,
    odd,
    halves,
    load_sem,
    vox_sem,
    face_send,
    face_recv,
    strip_send,
    strip_recv,
    rs_send,
    rs_recv,
    ag_send,
    ag_recv,
):
    me = lax.axis_index("gx")
    length, channels = voxels.shape[1], voxels.shape[2]
    depth = prior.shape[1]
    tiles = length // tile
    has_left, has_right = me > 0, me < n - 1
    left, right = me - 1, me + 1
    across = length // depth

    def across_bits(distance, hop):
        other, weight = me, 1
        while weight <= hop:
            bit = (me // (distance * weight)) % 2
            if hop & weight:
                other = other + (1 - 2 * bit) * distance * weight
            weight *= 2
        return other

    digits = [(me // distance) % radix for distance, radix, _, _ in stages]
    partners = []
    for distance, radix, _, _ in stages:
        found = {}
        for hop in range(1, radix):
            other = across_bits(distance, hop)
            found[hop] = (other, (other // distance) % radix)
        partners.append(found)
    slots = [sum(stage[1] - 1 for stage in stages[:k]) for k in range(len(stages))]
    far = [across_bits(2, hop) for hop in range(1, far_radix(stages))]

    taps = conv_first.shape[1]
    loads = []
    for source, target in ((conv_first, w_first), (conv_second, w_second)):
        for layer in range(2):
            for result in range(2):
                block = (pl.ds(layer * taps, taps), pl.ds(result * channels, channels))
                loads.append((source.at[1 + layer - result], target.at[block]))
    loads += [
        (score_x, w_score.at[:, pl.ds(0, channels)]),
        (score_y, w_score.at[:, pl.ds(channels, channels)]),
        (plane_yz_w, w_yz),
        (plane_xz_w, w_xz),
        (mlp_in, w_in),
        (mlp_out, w_out),
    ]
    vox_loads = [
        pltpu.make_async_copy(
            voxels.at[row], vox.at[row, pl.ds(PAD, length), :], vox_sem.at[row]
        )
        for row in range(2)
    ]
    loads = [
        pltpu.make_async_copy(source, target, load_sem.at[i])
        for i, (source, target) in enumerate(loads)
    ]
    for copy in vox_loads + loads:
        copy.start()

    barrier = pltpu.get_barrier_semaphore()
    greeted = far + [
        partner
        for stage, found in zip(stages, partners)
        for partner, _ in found.values()
        if stage[0] == 1 or not stage[3]
    ]
    for partner in greeted:
        pl.semaphore_signal(barrier, inc=1, device_id={"gx": partner}, device_id_type=MESH)

    @pl.when(has_left)
    def _():
        pl.semaphore_signal(barrier, inc=1, device_id={"gx": left}, device_id_type=MESH)

    @pl.when(has_right)
    def _():
        pl.semaphore_signal(barrier, inc=1, device_id={"gx": right}, device_id_type=MESH)

    edge = jnp.zeros((2, PAD, channels), BF16)
    for padded in (vox, face_vox, first, face_first):
        padded[:, 0:PAD, :] = edge
        padded[:, PAD + length :, :] = edge
    pooled[0:PAD, :] = edge[0]
    pooled[PAD + length :, :] = edge[0]

    for side, has in ((0, has_left), (1, has_right)):

        @pl.when(jnp.logical_not(has))
        def _():
            blank = jnp.zeros((length, channels), BF16)
            face_vox[side, pl.ds(PAD, length), :] = blank
            face_first[side, pl.ds(PAD, length), :] = blank
            strip[3 * side] = jnp.zeros(strip.shape[1:], F32)

    pl.semaphore_wait(barrier, len(greeted) + jnp.where(has_left, 1, 0) + jnp.where(has_right, 1, 0))

    def face_copy(which, source, target, side, t, to):
        return pltpu.make_async_remote_copy(
            src_ref=source,
            dst_ref=target.at[1 - side, pl.ds(pl.multiple_of(PAD + t * tile, 16), tile), :],
            send_sem=face_send.at[which, side, t],
            recv_sem=face_recv.at[which, 1 - side, t],
            device_id={"gx": to},
            device_id_type=MESH,
        )

    def vox_copy(side, t):
        source = voxels.at[side, pl.ds(pl.multiple_of(t * tile, 16), tile), :]
        return face_copy(0, source, face_vox, side, t, (left, right)[side])

    def first_copy(side, t):
        source = first.at[side, pl.ds(pl.multiple_of(PAD + t * tile, 16), tile), :]
        return face_copy(1, source, face_first, side, t, (left, right)[side])

    def arrive(make, side, t, has):
        @pl.when(has)
        def _():
            make(1 - side, t).wait_recv()

    def sent(make):
        for side, has in ((0, has_left), (1, has_right)):

            @pl.when(has)
            def _():
                for t in range(tiles):
                    make(side, t).wait_send()

    for t in range(tiles):
        for side, has in ((0, has_left), (1, has_right)):

            @pl.when(has)
            def _():
                vox_copy(side, t).start()

    def stack_tile(layer, source, t):
        stack(source, even.at[layer], odd.at[layer], PAD + t * tile, tile, depth)

    def stack_end(layer, source):
        stack(source, even.at[layer], odd.at[layer], PAD + length, PAD, depth)

    def around(layer, t):
        return neighbourhood(even.at[layer], odd.at[layer], PAD + t * tile, tile)

    def tile_at(t, offset=0):
        return pl.ds(pl.multiple_of(offset + t * tile, 16), tile)

    def inner(base, weight, t):
        both = jnp.concatenate([around(base, t), around(base + 1, t)], axis=1)
        acc[tile_at(t), :] = dot(both, weight[...])

    def face_tile(base, face, make, t):
        for side, has in ((0, has_left), (1, has_right)):
            arrive(make, side, t, has)
            stack_tile(base + 2 + side, face.at[side], t)

    def outer(base, weight, side, t):
        if side == 0:
            part = weight[:taps, channels:]
        else:
            part = weight[taps:, :channels]
        return acc[tile_at(t), side * channels : (side + 1) * channels] + dot(
            around(base + 2 + side, t), part
        )

    def repeat(count, body):
        def step(t, carry):
            body(t)
            return carry

        lax.fori_loop(0, count, step, 0)

    cells = tile // depth
    cube = (cells, depth, across)

    def spread_tile(t):
        lane = lax.broadcasted_iota(jnp.int32, cube, 2)
        cell = lax.broadcasted_iota(jnp.int32, cube, 0) + t * cells
        for side in range(2):
            field = jnp.broadcast_to(prior[side][None], cube)
            field = jnp.sum(jnp.where(lane == cell, field, 0.0), axis=2, keepdims=True)
            field = jnp.broadcast_to(field, (cells, depth, channels))
            spread[side, tile_at(t), :] = field.reshape(tile, channels)

    for copy in vox_loads + loads[:4]:
        copy.wait()

    @functools.partial(repeat, tiles + 1)
    def _(t):
        @pl.when(t < tiles)
        def _():
            for side in range(2):
                stack_tile(side, vox.at[side], t)

        @pl.when(t == tiles)
        def _():
            for side in range(2):
                stack_end(side, vox.at[side])

        @pl.when(t >= 1)
        def _():
            spread_tile(t - 1)
            inner(0, w_first, t - 1)

    for copy in loads[4:]:
        copy.wait()

    @functools.partial(repeat, tiles + 2)
    def _(t):
        @pl.when(t < tiles)
        def _():
            face_tile(0, face_vox, vox_copy, t)

        @pl.when(t == tiles)
        def _():
            for side in range(2):
                stack_end(2 + side, face_vox.at[side])

        @pl.when(jnp.logical_and(t >= 1, t <= tiles))
        def _():
            u = t - 1
            for side, has in ((0, has_left), (1, has_right)):
                value = activate(outer(0, w_first, side, u)).astype(BF16)
                first[side, tile_at(u, PAD), :] = value

                @pl.when(has)
                def _():
                    first_copy(side, u).start()

            for side in range(2):
                stack_tile(4 + side, first.at[side], u)

        @pl.when(t == tiles)
        def _():
            for side in range(2):
                stack_end(4 + side, first.at[side])

        @pl.when(t >= 2)
        def _():
            inner(4, w_second, t - 2)

    running[:, 0] = jnp.full((2, depth, channels), -jnp.inf, F32)
    running[:, 1:] = jnp.zeros((2, 2, depth, channels), F32)

    def local_part(t):
        logits, features = [], []
        for side in range(2):
            value = outer(4, w_second, side, t)
            value += vox[side, tile_at(t, PAD), :].astype(F32)
            value = value.astype(BF16)
            feature[side, tile_at(t), :] = value
            both = dot(value, w_score[...])
            field = spread[side, tile_at(t), :]
            value = value.astype(F32)
            logits.append(both[:, :channels] + field)
            features.append(value)
            logit_y = (both[:, channels:] + field).reshape(cells, depth, channels)
            value = value.reshape(cells, depth, channels)
            old, norm, total = running[side, 0], running[side, 1], running[side, 2]
            peak = jnp.maximum(jnp.max(logit_y, axis=0), old)
            weight = jnp.exp(logit_y - peak[None])
            keep = jnp.exp(old - peak)
            running[side, 0] = peak
            running[side, 1] = norm * keep + jnp.sum(weight, 0)
            running[side, 2] = total * keep + jnp.sum(weight * value, 0)
        peak = jnp.maximum(logits[0], logits[1]).astype(BF16)
        weights = [jnp.exp(logit - peak.astype(F32)) for logit in logits]
        stats[0, tile_at(t), :] = peak
        stats[1, tile_at(t), :] = (weights[0] + weights[1]).astype(BF16)
        stats[2, tile_at(t), :] = (weights[0] * features[0] + weights[1] * features[1]).astype(BF16)

    def rows_at(start, rows):
        return pl.ds(pl.multiple_of(start, 16), rows)

    def start_of(g, k):
        start = g * tile
        for digit, (_, _, rows, shares) in zip(digits[:k], stages):
            if shares:
                start = start + digit * rows
        return start

    def reduce_copies(g, k):
        distance, radix, rows, shares = stages[k]
        copies = []
        for hop in range(1, radix):
            partner, theirs = partners[k][hop]
            give = start_of(g, k)
            if shares:
                give = give + theirs * rows
            copies.append(
                pltpu.make_async_remote_copy(
                    src_ref=stats.at[:, rows_at(give, rows), :],
                    dst_ref=halves[k].at[g, hop - 1],
                    send_sem=rs_send.at[g, slots[k] + hop - 1],
                    recv_sem=rs_recv.at[g, slots[k] + hop - 1],
                    device_id={"gx": partner},
                    device_id_type=MESH,
                )
            )
        return copies

    def reduce_end(g, k):
        distance, radix, rows, shares = stages[k]
        for copy in reduce_copies(g, k):
            copy.wait_recv()
            if not shares:
                copy.wait_send()
        start = start_of(g, k + 1)
        at = rows_at(start, rows)
        held = [stats[:, at, :].astype(F32)]
        held += [halves[k][g, hop].astype(F32) for hop in range(radix - 1)]
        peak = functools.reduce(jnp.maximum, [each[0] for each in held])
        scales = [jnp.exp(each[0] - peak) for each in held]
        norm = sum(each[1] * scale for each, scale in zip(held, scales))
        total = sum(each[2] * scale for each, scale in zip(held, scales))
        if k + 1 < len(stages):
            for i, value in enumerate((peak, norm, total)):
                stats[i, at, :] = value.astype(BF16)
        else:
            pooled[rows_at(PAD + start, rows), :] = (total / norm).astype(BF16)

    def gather_copy(g, slot, start, rows, partner):
        part = pooled.at[rows_at(PAD + start, rows), :]
        return pltpu.make_async_remote_copy(
            src_ref=part,
            dst_ref=part,
            send_sem=ag_send.at[g, slot],
            recv_sem=ag_recv.at[g, slot],
            device_id={"gx": partner},
            device_id_type=MESH,
        )

    def far_copies(g):
        start, rows = start_of(g, len(stages)), stages[-1][2]
        return [gather_copy(g, i, start, rows, partner) for i, partner in enumerate(far)]

    def near_copies(g):
        rows = stages[0][2]
        return [gather_copy(g, len(far), start_of(g, 1), rows, partners[0][1][0])]

    def strip_copy(side):
        return pltpu.make_async_remote_copy(
            src_ref=strip.at[1 + side],
            dst_ref=strip.at[3 - 3 * side],
            send_sem=strip_send.at[side],
            recv_sem=strip_recv.at[1 - side],
            device_id={"gx": (left, right)[side]},
            device_id_type=MESH,
        )

    def strip_start():
        for side, has in ((0, has_left), (1, has_right)):
            strip[1 + side] = (running[side, 2] / running[side, 1]).astype(BF16).astype(F32)

            @pl.when(has)
            def _():
                strip_copy(side).start()

    def strip_plane():
        for side, has in ((0, has_left), (1, has_right)):

            @pl.when(has)
            def _():
                strip_copy(1 - side).wait_recv()

        moved = shifted(strip[...])
        stacked = [
            jnp.concatenate([part[x + i] for i in range(3) for part in moved], axis=1)
            for x in range(2)
        ]
        plane = dot(jnp.concatenate(stacked, axis=0).astype(BF16), w_xz[...])
        plane_xz[...] = plane.astype(BF16).astype(F32)

    def finish(t):
        plane_yz = dot(around(8, t), w_yz[...])
        plane_yz = plane_yz.astype(BF16).astype(F32).reshape(cells, depth, channels)
        for side in range(2):
            mixing = plane_yz + plane_xz[side * depth : (side + 1) * depth, :][None]
            joined = feature[side, tile_at(t), :].astype(F32) * mixing.reshape(tile, channels)
            squares = dot((joined * joined).astype(BF16), jnp.ones((channels, channels), BF16))
            scale = lax.rsqrt(squares * (1.0 / channels) + 1e-06)
            normed = (joined * scale * norm_gain[...]).astype(BF16)
            hidden = activate(dot(normed, w_in[...])).astype(BF16)
            out[side, tile_at(t), :] = (joined + dot(hidden, w_out[...])).astype(BF16)

    last = len(stages)

    @functools.partial(repeat, tiles + last + 4)
    def _(slot):
        @pl.when(slot < tiles)
        def _():
            face_tile(4, face_first, first_copy, slot)

        @pl.when(slot == tiles)
        def _():
            for side in range(2):
                stack_end(6 + side, face_first.at[side])

        @pl.when(jnp.logical_and(slot >= 1, slot <= tiles))
        def _():
            local_part(slot - 1)

        def at_step(step, body):
            g = slot - 1 - step

            @pl.when(jnp.logical_and(g >= 0, g < tiles))
            def _():
                body(g)

        def start_all(copies):
            for copy in copies:
                copy.start()

        def end_all(copies):
            for copy in copies:
                copy.wait_recv()

        def advance(k, g):
            if k > 0:
                reduce_end(g, k - 1)
            start_all(reduce_copies(g, k) if k < last else far_copies(g))

        def gather_near(g):
            end_all(far_copies(g))
            start_all(near_copies(g))

        def gather_end(g):
            end_all(near_copies(g))
            stack_tile(8, pooled, g)

            @pl.when(g == tiles - 1)
            def _():
                stack_end(8, pooled)

        for k in range(last + 1):
            at_step(k, functools.partial(advance, k))
        at_step(last + 1, gather_near)
        at_step(last + 2, gather_end)

        @pl.when(slot == tiles)
        def _():
            strip_start()

        @pl.when(slot == tiles + 1)
        def _():
            strip_plane()

        at_step(last + 3, finish)

    @functools.partial(repeat, tiles)
    def _(g):
        for k, (_, _, _, shares) in enumerate(stages):
            for copy in reduce_copies(g, k) if shares else []:
                copy.wait_send()
        for copy in far_copies(g) + near_copies(g):
            copy.wait_send()

    sent(vox_copy)
    sent(first_copy)
    for side, has in ((0, has_left), (1, has_right)):

        @pl.when(has)
        def _():
            strip_copy(side).wait_send()


def on_device(
    n,
    voxels,
    prior,
    conv_first,
    conv_second,
    score_x,
    score_y,
    plane_yz_w,
    plane_xz_w,
    norm_gain,
    mlp_in,
    mlp_out,
):
    rows, across, depth, channels = voxels.shape
    assert rows == 2 and depth == 8 and n & (n - 1) == 0
    length = across * depth
    hidden = mlp_in.shape[1]
    tile = min(512, length)
    tiles = length // tile
    stages = stages_of(tile, n)
    exchanges = sum(stage[1] - 1 for stage in stages)
    padded = length + 2 * PAD
    taps = conv_first.shape[0] // 3 * channels
    hbm = pl.BlockSpec(memory_space=pl.ANY)
    vmem = pl.BlockSpec(memory_space=pltpu.VMEM)
    result = pl.pallas_call(
        functools.partial(kernel, n, tile, stages),
        out_shape=jax.ShapeDtypeStruct((rows, length, channels), BF16),
        in_specs=[hbm, vmem, hbm, hbm, hbm, hbm, hbm, hbm, vmem, hbm, hbm],
        out_specs=vmem,
        scratch_shapes=[
            pltpu.VMEM((2 * taps, 2 * channels), BF16),
            pltpu.VMEM((2 * taps, 2 * channels), BF16),
            pltpu.VMEM((channels, 2 * channels), BF16),
            pltpu.VMEM((taps, channels), BF16),
            pltpu.VMEM((taps, channels), BF16),
            pltpu.VMEM((channels, hidden), BF16),
            pltpu.VMEM((hidden, channels), BF16),
            pltpu.VMEM((2, padded, channels), BF16),
            pltpu.VMEM((2, padded, channels), BF16),
            pltpu.VMEM((2, padded, channels), BF16),
            pltpu.VMEM((2, padded, channels), BF16),
            pltpu.VMEM((length, 2 * channels), F32),
            pltpu.VMEM((2, length, channels), BF16),
            pltpu.VMEM((3, length, channels), BF16),
            pltpu.VMEM((padded, channels), BF16),
            pltpu.VMEM((4, depth, channels), F32),
            pltpu.VMEM((2, 3, depth, channels), F32),
            pltpu.VMEM((2 * depth, channels), F32),
            pltpu.VMEM((2, length, channels), F32),
            pltpu.VMEM((9, padded, 3 * channels), BF16),
            pltpu.VMEM((9, padded, 3 * channels), BF16),
            [
                pltpu.VMEM((tiles, radix - 1, 3, share, channels), BF16)
                for _, radix, share, _ in stages
            ],
            pltpu.SemaphoreType.DMA((14,)),
            pltpu.SemaphoreType.DMA((2,)),
            pltpu.SemaphoreType.DMA((2, 2, tiles)),
            pltpu.SemaphoreType.DMA((2, 2, tiles)),
            pltpu.SemaphoreType.DMA((2,)),
            pltpu.SemaphoreType.DMA((2,)),
            pltpu.SemaphoreType.DMA((tiles, exchanges)),
            pltpu.SemaphoreType.DMA((tiles, exchanges)),
            pltpu.SemaphoreType.DMA((tiles, far_radix(stages))),
            pltpu.SemaphoreType.DMA((tiles, far_radix(stages))),
        ],
        compiler_params=pltpu.CompilerParams(
            collective_id=0, has_side_effects=True, vmem_limit_bytes=62 * 1024 * 1024
        ),
    )(
        voxels.reshape(rows, length, channels),
        prior.transpose(0, 2, 1),
        conv_first.reshape(3, taps, channels),
        conv_second.reshape(3, taps, channels),
        score_x,
        score_y,
        plane_yz_w.reshape(taps, channels),
        plane_xz_w.reshape(taps, channels),
        norm_gain.reshape(1, channels),
        mlp_in,
        mlp_out,
    )
    return result.reshape(voxels.shape)


def solution(mesh):
    split = P(("scene", "gx"), None, None, None)
    return jax.shard_map(
        functools.partial(on_device, mesh.shape["gx"]),
        mesh=mesh,
        in_specs=(split, P(("scene", "gx"), None, None)) + (P(),) * 9,
        out_specs=split,
        check_vma=False,
    )
```

```python
import functools

import jax
import jax.numpy as jnp
from jax import lax
from jax.experimental import pallas as pl
from jax.experimental.pallas import tpu as pltpu
from jax.sharding import PartitionSpec as P

MESH = pl.DeviceIdType.MESH
PAD = 16
F32 = jnp.float32
BF16 = jnp.bfloat16


def activate(values):
    return jax.nn.gelu(values, approximate=True)


def stages_of(rows, devices):
    count = devices.bit_length() - 1
    bits = [[0], list(range(1, min(4, count)))]
    bits += [list(range(i, min(i + 2, count))) for i in range(4, count, 2)]
    bits = [group for group in bits if group and group[-1] < count]
    stages = []
    for group in bits:
        radix = 1 << len(group)
        shares = rows % (16 * radix) == 0
        rows = rows // radix if shares else rows
        stages.append((1 << group[0], radix, rows, shares))
    return stages


def far_radix(stages):
    total = 1
    for distance, radix, _, shares in stages:
        if shares:
            total *= radix
    return total


def shifted(values):
    depth = values.shape[1]
    at_z = lax.broadcasted_iota(jnp.int32, (1,) + values.shape[1:], 1)
    below = jnp.where(at_z == 0, 0.0, pltpu.roll(values, 1, 1))
    above = jnp.where(at_z == depth - 1, 0.0, pltpu.roll(values, depth - 1, 1))
    return below, values, above


def stack(source, even, odd, start, rows, depth):
    channels = source.shape[1]
    window = source[pl.ds(pl.multiple_of(start - PAD, 16), rows + PAD), :].astype(F32)
    parts = shifted(window.reshape(-1, depth, channels))
    at = pl.ds(pl.multiple_of(start, 16), rows)
    for i, part in enumerate(parts):
        part = part.reshape(rows + PAD, channels)
        columns = slice(i * channels, (i + 1) * channels)
        even[at, columns] = part[PAD:].astype(BF16)
        odd[at, columns] = part[PAD - depth : rows + PAD - depth].astype(BF16)


def neighbourhood(even, odd, start, tile):
    first = pl.ds(pl.multiple_of(start, 16), tile)
    after = pl.ds(pl.multiple_of(start + PAD, 16), tile)
    return jnp.concatenate([odd[first, :], even[first, :], odd[after, :]], axis=1)


def dot(a, b):
    return jnp.dot(a, b, preferred_element_type=F32)


def kernel(
    n,
    tile,
    stages,
    voxels,
    prior,
    conv_first,
    conv_second,
    score_x,
    score_y,
    plane_yz_w,
    plane_xz_w,
    norm_gain,
    mlp_in,
    mlp_out,
    out,
    w_first,
    w_second,
    w_score,
    w_yz,
    w_xz,
    w_in,
    w_out,
    vox,
    face_vox,
    first,
    face_first,
    acc,
    feature,
    stats,
    pooled,
    strip,
    running,
    plane_xz,
    spread,
    even,
    odd,
    halves,
    load_sem,
    vox_sem,
    face_send,
    face_recv,
    strip_send,
    strip_recv,
    rs_send,
    rs_recv,
    ag_send,
    ag_recv,
):
    me = lax.axis_index("gx")
    length, channels = voxels.shape[1], voxels.shape[2]
    depth = prior.shape[1]
    tiles = length // tile
    has_left, has_right = me > 0, me < n - 1
    left, right = me - 1, me + 1
    across = length // depth

    def across_bits(distance, hop):
        other, weight = me, 1
        while weight <= hop:
            bit = (me // (distance * weight)) % 2
            if hop & weight:
                other = other + (1 - 2 * bit) * distance * weight
            weight *= 2
        return other

    digits = [(me // distance) % radix for distance, radix, _, _ in stages]
    partners = []
    for distance, radix, _, _ in stages:
        found = {}
        for hop in range(1, radix):
            other = across_bits(distance, hop)
            found[hop] = (other, (other // distance) % radix)
        partners.append(found)
    slots = [sum(stage[1] - 1 for stage in stages[:k]) for k in range(len(stages))]
    far = [across_bits(1, hop) for hop in range(1, far_radix(stages))]

    taps = conv_first.shape[1]
    loads = []
    for source, target in ((conv_first, w_first), (conv_second, w_second)):
        for layer in range(2):
            for result in range(2):
                block = (pl.ds(layer * taps, taps), pl.ds(result * channels, channels))
                loads.append((source.at[1 + layer - result], target.at[block]))
    loads += [
        (score_x, w_score.at[:, pl.ds(0, channels)]),
        (score_y, w_score.at[:, pl.ds(channels, channels)]),
        (plane_yz_w, w_yz),
        (plane_xz_w, w_xz),
        (mlp_in, w_in),
        (mlp_out, w_out),
    ]
    vox_loads = [
        pltpu.make_async_copy(
            voxels.at[row], vox.at[row, pl.ds(PAD, length), :], vox_sem.at[row]
        )
        for row in range(2)
    ]
    loads = [
        pltpu.make_async_copy(source, target, load_sem.at[i])
        for i, (source, target) in enumerate(loads)
    ]
    for copy in vox_loads + loads:
        copy.start()

    barrier = pltpu.get_barrier_semaphore()
    greeted = far + [
        partner
        for stage, found in zip(stages, partners)
        for partner, _ in found.values()
        if not stage[3]
    ]
    for partner in greeted:
        pl.semaphore_signal(barrier, inc=1, device_id={"gx": partner}, device_id_type=MESH)

    @pl.when(has_left)
    def _():
        pl.semaphore_signal(barrier, inc=1, device_id={"gx": left}, device_id_type=MESH)

    @pl.when(has_right)
    def _():
        pl.semaphore_signal(barrier, inc=1, device_id={"gx": right}, device_id_type=MESH)

    edge = jnp.zeros((2, PAD, channels), BF16)
    for padded in (vox, face_vox, first, face_first):
        padded[:, 0:PAD, :] = edge
        padded[:, PAD + length :, :] = edge
    pooled[0:PAD, :] = edge[0]
    pooled[PAD + length :, :] = edge[0]

    for side, has in ((0, has_left), (1, has_right)):

        @pl.when(jnp.logical_not(has))
        def _():
            blank = jnp.zeros((length, channels), BF16)
            face_vox[side, pl.ds(PAD, length), :] = blank
            face_first[side, pl.ds(PAD, length), :] = blank
            strip[3 * side] = jnp.zeros(strip.shape[1:], F32)

    pl.semaphore_wait(barrier, len(greeted) + jnp.where(has_left, 1, 0) + jnp.where(has_right, 1, 0))

    def face_copy(which, source, target, side, t, to):
        return pltpu.make_async_remote_copy(
            src_ref=source,
            dst_ref=target.at[1 - side, pl.ds(pl.multiple_of(PAD + t * tile, 16), tile), :],
            send_sem=face_send.at[which, side, t],
            recv_sem=face_recv.at[which, 1 - side, t],
            device_id={"gx": to},
            device_id_type=MESH,
        )

    def vox_copy(side, t):
        source = voxels.at[side, pl.ds(pl.multiple_of(t * tile, 16), tile), :]
        return face_copy(0, source, face_vox, side, t, (left, right)[side])

    def first_copy(side, t):
        source = first.at[side, pl.ds(pl.multiple_of(PAD + t * tile, 16), tile), :]
        return face_copy(1, source, face_first, side, t, (left, right)[side])

    def arrive(make, side, t, has):
        @pl.when(has)
        def _():
            make(1 - side, t).wait_recv()

    def sent(make):
        for side, has in ((0, has_left), (1, has_right)):

            @pl.when(has)
            def _():
                for t in range(tiles):
                    make(side, t).wait_send()

    for t in range(tiles):
        for side, has in ((0, has_left), (1, has_right)):

            @pl.when(has)
            def _():
                vox_copy(side, t).start()

    def stack_tile(layer, source, t):
        stack(source, even.at[layer], odd.at[layer], PAD + t * tile, tile, depth)

    def stack_end(layer, source):
        stack(source, even.at[layer], odd.at[layer], PAD + length, PAD, depth)

    def around(layer, t):
        return neighbourhood(even.at[layer], odd.at[layer], PAD + t * tile, tile)

    def tile_at(t, offset=0):
        return pl.ds(pl.multiple_of(offset + t * tile, 16), tile)

    def inner(base, weight, t):
        both = jnp.concatenate([around(base, t), around(base + 1, t)], axis=1)
        acc[tile_at(t), :] = dot(both, weight[...])

    def face_tile(base, face, make, t):
        for side, has in ((0, has_left), (1, has_right)):
            arrive(make, side, t, has)
            stack_tile(base + 2 + side, face.at[side], t)

    def outer(base, weight, side, t):
        if side == 0:
            part = weight[:taps, channels:]
        else:
            part = weight[taps:, :channels]
        return acc[tile_at(t), side * channels : (side + 1) * channels] + dot(
            around(base + 2 + side, t), part
        )

    def repeat(count, body):
        def step(t, carry):
            body(t)
            return carry

        lax.fori_loop(0, count, step, 0)

    cells = tile // depth
    cube = (cells, depth, across)

    def spread_tile(t):
        lane = lax.broadcasted_iota(jnp.int32, cube, 2)
        cell = lax.broadcasted_iota(jnp.int32, cube, 0) + t * cells
        for side in range(2):
            field = jnp.broadcast_to(prior[side][None], cube)
            field = jnp.sum(jnp.where(lane == cell, field, 0.0), axis=2, keepdims=True)
            field = jnp.broadcast_to(field, (cells, depth, channels))
            spread[side, tile_at(t), :] = field.reshape(tile, channels)

    for copy in vox_loads + loads[:4]:
        copy.wait()

    @functools.partial(repeat, tiles + 1)
    def _(t):
        @pl.when(t < tiles)
        def _():
            for side in range(2):
                stack_tile(side, vox.at[side], t)

        @pl.when(t == tiles)
        def _():
            for side in range(2):
                stack_end(side, vox.at[side])

        @pl.when(t >= 1)
        def _():
            spread_tile(t - 1)
            inner(0, w_first, t - 1)

    for copy in loads[4:]:
        copy.wait()

    @functools.partial(repeat, tiles + 2)
    def _(t):
        @pl.when(t < tiles)
        def _():
            face_tile(0, face_vox, vox_copy, t)

        @pl.when(t == tiles)
        def _():
            for side in range(2):
                stack_end(2 + side, face_vox.at[side])

        @pl.when(jnp.logical_and(t >= 1, t <= tiles))
        def _():
            u = t - 1
            for side, has in ((0, has_left), (1, has_right)):
                value = activate(outer(0, w_first, side, u)).astype(BF16)
                first[side, tile_at(u, PAD), :] = value

                @pl.when(has)
                def _():
                    first_copy(side, u).start()

            for side in range(2):
                stack_tile(4 + side, first.at[side], u)

        @pl.when(t == tiles)
        def _():
            for side in range(2):
                stack_end(4 + side, first.at[side])

        @pl.when(t >= 2)
        def _():
            inner(4, w_second, t - 2)

    running[:, 0] = jnp.full((2, depth, channels), -jnp.inf, F32)
    running[:, 1:] = jnp.zeros((2, 2, depth, channels), F32)

    def local_part(t):
        logits, features = [], []
        for side in range(2):
            value = outer(4, w_second, side, t)
            value += vox[side, tile_at(t, PAD), :].astype(F32)
            value = value.astype(BF16)
            feature[side, tile_at(t), :] = value
            both = dot(value, w_score[...])
            field = spread[side, tile_at(t), :]
            value = value.astype(F32)
            logits.append(both[:, :channels] + field)
            features.append(value)
            logit_y = (both[:, channels:] + field).reshape(cells, depth, channels)
            value = value.reshape(cells, depth, channels)
            old, norm, total = running[side, 0], running[side, 1], running[side, 2]
            peak = jnp.maximum(jnp.max(logit_y, axis=0), old)
            weight = jnp.exp(logit_y - peak[None])
            keep = jnp.exp(old - peak)
            running[side, 0] = peak
            running[side, 1] = norm * keep + jnp.sum(weight, 0)
            running[side, 2] = total * keep + jnp.sum(weight * value, 0)
        peak = jnp.maximum(logits[0], logits[1]).astype(BF16)
        weights = [jnp.exp(logit - peak.astype(F32)) for logit in logits]
        stats[0, tile_at(t), :] = peak
        stats[1, tile_at(t), :] = (weights[0] + weights[1]).astype(BF16)
        stats[2, tile_at(t), :] = (weights[0] * features[0] + weights[1] * features[1]).astype(BF16)

    def rows_at(start, rows):
        return pl.ds(pl.multiple_of(start, 16), rows)

    def start_of(g, k):
        start = g * tile
        for digit, (_, _, rows, shares) in zip(digits[:k], stages):
            if shares:
                start = start + digit * rows
        return start

    def reduce_copies(g, k):
        distance, radix, rows, shares = stages[k]
        copies = []
        for hop in range(1, radix):
            partner, theirs = partners[k][hop]
            give = start_of(g, k)
            if shares:
                give = give + theirs * rows
            copies.append(
                pltpu.make_async_remote_copy(
                    src_ref=stats.at[:, rows_at(give, rows), :],
                    dst_ref=halves[k].at[g, hop - 1],
                    send_sem=rs_send.at[g, slots[k] + hop - 1],
                    recv_sem=rs_recv.at[g, slots[k] + hop - 1],
                    device_id={"gx": partner},
                    device_id_type=MESH,
                )
            )
        return copies

    def reduce_end(g, k):
        distance, radix, rows, shares = stages[k]
        for copy in reduce_copies(g, k):
            copy.wait_recv()
            if not shares:
                copy.wait_send()
        start = start_of(g, k + 1)
        at = rows_at(start, rows)
        held = [stats[:, at, :].astype(F32)]
        held += [halves[k][g, hop].astype(F32) for hop in range(radix - 1)]
        peak = functools.reduce(jnp.maximum, [each[0] for each in held])
        scales = [jnp.exp(each[0] - peak) for each in held]
        norm = sum(each[1] * scale for each, scale in zip(held, scales))
        total = sum(each[2] * scale for each, scale in zip(held, scales))
        if k + 1 < len(stages):
            for i, value in enumerate((peak, norm, total)):
                stats[i, at, :] = value.astype(BF16)
        else:
            pooled[rows_at(PAD + start, rows), :] = (total / norm).astype(BF16)

    def gather_copy(g, slot, start, rows, partner):
        part = pooled.at[rows_at(PAD + start, rows), :]
        return pltpu.make_async_remote_copy(
            src_ref=part,
            dst_ref=part,
            send_sem=ag_send.at[g, slot],
            recv_sem=ag_recv.at[g, slot],
            device_id={"gx": partner},
            device_id_type=MESH,
        )

    def far_copies(g):
        start, rows = start_of(g, len(stages)), stages[-1][2]
        return [gather_copy(g, i, start, rows, partner) for i, partner in enumerate(far)]

    def strip_copy(side):
        return pltpu.make_async_remote_copy(
            src_ref=strip.at[1 + side],
            dst_ref=strip.at[3 - 3 * side],
            send_sem=strip_send.at[side],
            recv_sem=strip_recv.at[1 - side],
            device_id={"gx": (left, right)[side]},
            device_id_type=MESH,
        )

    def strip_start():
        for side, has in ((0, has_left), (1, has_right)):
            strip[1 + side] = (running[side, 2] / running[side, 1]).astype(BF16).astype(F32)

            @pl.when(has)
            def _():
                strip_copy(side).start()

    def strip_plane():
        for side, has in ((0, has_left), (1, has_right)):

            @pl.when(has)
            def _():
                strip_copy(1 - side).wait_recv()

        moved = shifted(strip[...])
        stacked = [
            jnp.concatenate([part[x + i] for i in range(3) for part in moved], axis=1)
            for x in range(2)
        ]
        plane = dot(jnp.concatenate(stacked, axis=0).astype(BF16), w_xz[...])
        plane_xz[...] = plane.astype(BF16).astype(F32)

    def finish(t):
        plane_yz = dot(around(8, t), w_yz[...])
        plane_yz = plane_yz.astype(BF16).astype(F32).reshape(cells, depth, channels)
        for side in range(2):
            mixing = plane_yz + plane_xz[side * depth : (side + 1) * depth, :][None]
            joined = feature[side, tile_at(t), :].astype(F32) * mixing.reshape(tile, channels)
            squares = dot((joined * joined).astype(BF16), jnp.ones((channels, channels), BF16))
            scale = lax.rsqrt(squares * (1.0 / channels) + 1e-06)
            normed = (joined * scale * norm_gain[...]).astype(BF16)
            hidden = activate(dot(normed, w_in[...])).astype(BF16)
            out[side, tile_at(t), :] = (joined + dot(hidden, w_out[...])).astype(BF16)

    last = len(stages)

    @functools.partial(repeat, tiles + last + 3)
    def _(slot):
        @pl.when(slot < tiles)
        def _():
            face_tile(4, face_first, first_copy, slot)

        @pl.when(slot == tiles)
        def _():
            for side in range(2):
                stack_end(6 + side, face_first.at[side])

        @pl.when(jnp.logical_and(slot >= 1, slot <= tiles))
        def _():
            local_part(slot - 1)

        def at_step(step, body):
            g = slot - 1 - step

            @pl.when(jnp.logical_and(g >= 0, g < tiles))
            def _():
                body(g)

        def start_all(copies):
            for copy in copies:
                copy.start()

        def end_all(copies):
            for copy in copies:
                copy.wait_recv()

        def advance(k, g):
            if k > 0:
                reduce_end(g, k - 1)
            start_all(reduce_copies(g, k) if k < last else far_copies(g))

        def gather_end(g):
            end_all(far_copies(g))
            stack_tile(8, pooled, g)

            @pl.when(g == tiles - 1)
            def _():
                stack_end(8, pooled)

        for k in range(last + 1):
            at_step(k, functools.partial(advance, k))
        at_step(last + 1, gather_end)

        @pl.when(slot == tiles)
        def _():
            strip_start()

        @pl.when(slot == tiles + 1)
        def _():
            strip_plane()

        at_step(last + 2, finish)

    @functools.partial(repeat, tiles)
    def _(g):
        for k, (_, _, _, shares) in enumerate(stages):
            for copy in reduce_copies(g, k) if shares else []:
                copy.wait_send()
        for copy in far_copies(g):
            copy.wait_send()

    sent(vox_copy)
    sent(first_copy)
    for side, has in ((0, has_left), (1, has_right)):

        @pl.when(has)
        def _():
            strip_copy(side).wait_send()


def on_device(
    n,
    voxels,
    prior,
    conv_first,
    conv_second,
    score_x,
    score_y,
    plane_yz_w,
    plane_xz_w,
    norm_gain,
    mlp_in,
    mlp_out,
):
    rows, across, depth, channels = voxels.shape
    assert rows == 2 and depth == 8 and n & (n - 1) == 0
    length = across * depth
    hidden = mlp_in.shape[1]
    tile = min(256, length)
    tiles = length // tile
    stages = stages_of(tile, n)
    exchanges = sum(stage[1] - 1 for stage in stages)
    padded = length + 2 * PAD
    taps = conv_first.shape[0] // 3 * channels
    hbm = pl.BlockSpec(memory_space=pl.ANY)
    vmem = pl.BlockSpec(memory_space=pltpu.VMEM)
    result = pl.pallas_call(
        functools.partial(kernel, n, tile, stages),
        out_shape=jax.ShapeDtypeStruct((rows, length, channels), BF16),
        in_specs=[hbm, vmem, hbm, hbm, hbm, hbm, hbm, hbm, vmem, hbm, hbm],
        out_specs=vmem,
        scratch_shapes=[
            pltpu.VMEM((2 * taps, 2 * channels), BF16),
            pltpu.VMEM((2 * taps, 2 * channels), BF16),
            pltpu.VMEM((channels, 2 * channels), BF16),
            pltpu.VMEM((taps, channels), BF16),
            pltpu.VMEM((taps, channels), BF16),
            pltpu.VMEM((channels, hidden), BF16),
            pltpu.VMEM((hidden, channels), BF16),
            pltpu.VMEM((2, padded, channels), BF16),
            pltpu.VMEM((2, padded, channels), BF16),
            pltpu.VMEM((2, padded, channels), BF16),
            pltpu.VMEM((2, padded, channels), BF16),
            pltpu.VMEM((length, 2 * channels), F32),
            pltpu.VMEM((2, length, channels), BF16),
            pltpu.VMEM((3, length, channels), BF16),
            pltpu.VMEM((padded, channels), BF16),
            pltpu.VMEM((4, depth, channels), F32),
            pltpu.VMEM((2, 3, depth, channels), F32),
            pltpu.VMEM((2 * depth, channels), F32),
            pltpu.VMEM((2, length, channels), F32),
            pltpu.VMEM((9, padded, 3 * channels), BF16),
            pltpu.VMEM((9, padded, 3 * channels), BF16),
            [
                pltpu.VMEM((tiles, radix - 1, 3, share, channels), BF16)
                for _, radix, share, _ in stages
            ],
            pltpu.SemaphoreType.DMA((14,)),
            pltpu.SemaphoreType.DMA((2,)),
            pltpu.SemaphoreType.DMA((2, 2, tiles)),
            pltpu.SemaphoreType.DMA((2, 2, tiles)),
            pltpu.SemaphoreType.DMA((2,)),
            pltpu.SemaphoreType.DMA((2,)),
            pltpu.SemaphoreType.DMA((tiles, exchanges)),
            pltpu.SemaphoreType.DMA((tiles, exchanges)),
            pltpu.SemaphoreType.DMA((tiles, far_radix(stages))),
            pltpu.SemaphoreType.DMA((tiles, far_radix(stages))),
        ],
        compiler_params=pltpu.CompilerParams(
            collective_id=0, has_side_effects=True, vmem_limit_bytes=62 * 1024 * 1024
        ),
    )(
        voxels.reshape(rows, length, channels),
        prior.transpose(0, 2, 1),
        conv_first.reshape(3, taps, channels),
        conv_second.reshape(3, taps, channels),
        score_x,
        score_y,
        plane_yz_w.reshape(taps, channels),
        plane_xz_w.reshape(taps, channels),
        norm_gain.reshape(1, channels),
        mlp_in,
        mlp_out,
    )
    return result.reshape(voxels.shape)


def solution(mesh):
    split = P(("scene", "gx"), None, None, None)
    return jax.shard_map(
        functools.partial(on_device, mesh.shape["gx"]),
        mesh=mesh,
        in_specs=(split, P(("scene", "gx"), None, None)) + (P(),) * 9,
        out_specs=split,
        check_vma=False,
    )
```

```python
import functools

import jax
import jax.numpy as jnp
from jax import lax
from jax.experimental import pallas as pl
from jax.experimental.pallas import tpu as pltpu
from jax.sharding import PartitionSpec as P

MESH = pl.DeviceIdType.MESH
PAD = 16
F32 = jnp.float32
BF16 = jnp.bfloat16


def activate(values):
    return jax.nn.gelu(values, approximate=True)


def stages_of(rows, devices):
    count = devices.bit_length() - 1
    bits = [[0], list(range(1, min(4, count)))]
    bits += [list(range(i, min(i + 2, count))) for i in range(4, count, 2)]
    bits = [group for group in bits if group and group[-1] < count]
    stages = []
    for group in bits:
        radix = 1 << len(group)
        shares = rows % (16 * radix) == 0
        rows = rows // radix if shares else rows
        stages.append((1 << group[0], radix, rows, shares))
    return stages


def far_radix(stages):
    total = 1
    for distance, radix, _, shares in stages:
        if shares:
            total *= radix
    return total


def shifted(values):
    depth = values.shape[1]
    at_z = lax.broadcasted_iota(jnp.int32, (1,) + values.shape[1:], 1)
    below = jnp.where(at_z == 0, 0.0, pltpu.roll(values, 1, 1))
    above = jnp.where(at_z == depth - 1, 0.0, pltpu.roll(values, depth - 1, 1))
    return below, values, above


def stack(source, even, odd, start, rows, depth):
    channels = source.shape[1]
    window = source[pl.ds(pl.multiple_of(start - PAD, 16), rows + PAD), :].astype(F32)
    parts = shifted(window.reshape(-1, depth, channels))
    at = pl.ds(pl.multiple_of(start, 16), rows)
    for i, part in enumerate(parts):
        part = part.reshape(rows + PAD, channels)
        columns = slice(i * channels, (i + 1) * channels)
        even[at, columns] = part[PAD:].astype(BF16)
        odd[at, columns] = part[PAD - depth : rows + PAD - depth].astype(BF16)


def neighbourhood(even, odd, start, tile):
    first = pl.ds(pl.multiple_of(start, 16), tile)
    after = pl.ds(pl.multiple_of(start + PAD, 16), tile)
    return jnp.concatenate([odd[first, :], even[first, :], odd[after, :]], axis=1)


def dot(a, b):
    return jnp.dot(a, b, preferred_element_type=F32)


def kernel(
    n,
    tile,
    stages,
    voxels,
    prior,
    conv_first,
    conv_second,
    score_x,
    score_y,
    plane_yz_w,
    plane_xz_w,
    norm_gain,
    mlp_in,
    mlp_out,
    out,
    w_first,
    w_second,
    w_face,
    w_score,
    w_yz,
    w_xz,
    w_in,
    w_out,
    vox,
    face_vox,
    first,
    face_first,
    acc,
    feature,
    stats,
    pooled,
    strip,
    running,
    plane_xz,
    spread,
    even,
    odd,
    halves,
    load_sem,
    vox_sem,
    face_send,
    face_recv,
    strip_send,
    strip_recv,
    rs_send,
    rs_recv,
    ag_send,
    ag_recv,
):
    me = lax.axis_index("gx")
    length, channels = voxels.shape[1], voxels.shape[2]
    depth = prior.shape[1]
    tiles = length // tile
    has_left, has_right = me > 0, me < n - 1
    left, right = me - 1, me + 1
    across = length // depth

    def across_bits(distance, hop):
        other, weight = me, 1
        while weight <= hop:
            bit = (me // (distance * weight)) % 2
            if hop & weight:
                other = other + (1 - 2 * bit) * distance * weight
            weight *= 2
        return other

    digits = [(me // distance) % radix for distance, radix, _, _ in stages]
    partners = []
    for distance, radix, _, _ in stages:
        found = {}
        for hop in range(1, radix):
            other = across_bits(distance, hop)
            found[hop] = (other, (other // distance) % radix)
        partners.append(found)
    slots = [sum(stage[1] - 1 for stage in stages[:k]) for k in range(len(stages))]
    far = [across_bits(1, hop) for hop in range(1, far_radix(stages))]

    taps = conv_first.shape[1]
    loads = []
    wide, third = 2 * taps // 3, taps // 3

    def paired(source, target):
        return [
            (source.at[pl.ds(0, wide)], target.at[:, pl.ds(0, channels)]),
            (source.at[pl.ds(wide, third)], target.at[pl.ds(third, third), pl.ds(channels, channels)]),
        ]

    for i, (source, target) in enumerate(((conv_first, w_first), (conv_second, w_second))):
        for side in range(2):
            loads += paired(source.at[2 * side], w_face.at[i, side])
        for layer in range(2):
            for result in range(2):
                block = (pl.ds(layer * taps, taps), pl.ds(result * channels, channels))
                loads.append((source.at[1 + layer - result], target.at[block]))
    loads += [
        (score_x, w_score.at[:, pl.ds(0, channels)]),
        (score_y, w_score.at[:, pl.ds(channels, channels)]),
        (plane_xz_w, w_xz),
        (mlp_in, w_in),
        (mlp_out, w_out),
    ]
    loads += paired(plane_yz_w, w_yz)
    vox_loads = [
        pltpu.make_async_copy(
            voxels.at[row], vox.at[row, pl.ds(PAD, length), :], vox_sem.at[row]
        )
        for row in range(2)
    ]
    loads = [
        pltpu.make_async_copy(source, target, load_sem.at[i])
        for i, (source, target) in enumerate(loads)
    ]
    for copy in vox_loads + loads:
        copy.start()

    barrier = pltpu.get_barrier_semaphore()
    greeted = far + [
        partner
        for stage, found in zip(stages, partners)
        for partner, _ in found.values()
        if not stage[3]
    ]
    for partner in greeted:
        pl.semaphore_signal(barrier, inc=1, device_id={"gx": partner}, device_id_type=MESH)

    @pl.when(has_left)
    def _():
        pl.semaphore_signal(barrier, inc=1, device_id={"gx": left}, device_id_type=MESH)

    @pl.when(has_right)
    def _():
        pl.semaphore_signal(barrier, inc=1, device_id={"gx": right}, device_id_type=MESH)

    w_face[:, :, :third, channels:] = jnp.zeros((2, 2, third, channels), BF16)
    w_yz[:third, channels:] = jnp.zeros((third, channels), BF16)
    edge = jnp.zeros((2, PAD, channels), BF16)
    for padded in (vox, face_vox, first, face_first):
        padded[:, 0:PAD, :] = edge
        padded[:, PAD + length :, :] = edge
    pooled[0:PAD, :] = edge[0]
    pooled[PAD + length :, :] = edge[0]

    for side, has in ((0, has_left), (1, has_right)):

        @pl.when(jnp.logical_not(has))
        def _():
            blank = jnp.zeros((length, channels), BF16)
            face_vox[side, pl.ds(PAD, length), :] = blank
            face_first[side, pl.ds(PAD, length), :] = blank
            strip[3 * side] = jnp.zeros(strip.shape[1:], F32)

    pl.semaphore_wait(barrier, len(greeted) + jnp.where(has_left, 1, 0) + jnp.where(has_right, 1, 0))

    def face_copy(which, source, target, side, t, to):
        return pltpu.make_async_remote_copy(
            src_ref=source,
            dst_ref=target.at[1 - side, pl.ds(pl.multiple_of(PAD + t * tile, 16), tile), :],
            send_sem=face_send.at[which, side, t],
            recv_sem=face_recv.at[which, 1 - side, t],
            device_id={"gx": to},
            device_id_type=MESH,
        )

    def vox_copy(side, t):
        source = voxels.at[side, pl.ds(pl.multiple_of(t * tile, 16), tile), :]
        return face_copy(0, source, face_vox, side, t, (left, right)[side])

    def first_copy(side, t):
        source = first.at[side, pl.ds(pl.multiple_of(PAD + t * tile, 16), tile), :]
        return face_copy(1, source, face_first, side, t, (left, right)[side])

    def arrive(make, side, t, has):
        @pl.when(has)
        def _():
            make(1 - side, t).wait_recv()

    def sent(make):
        for side, has in ((0, has_left), (1, has_right)):

            @pl.when(has)
            def _():
                for t in range(tiles):
                    make(side, t).wait_send()

    for t in range(tiles):
        for side, has in ((0, has_left), (1, has_right)):

            @pl.when(has)
            def _():
                vox_copy(side, t).start()

    def stack_tile(layer, source, t):
        stack(source, even.at[layer], odd.at[layer], PAD + t * tile, tile, depth)

    def stack_end(layer, source):
        stack(source, even.at[layer], odd.at[layer], PAD + length, PAD, depth)

    def around(layer, t):
        return neighbourhood(even.at[layer], odd.at[layer], PAD + t * tile, tile)

    def tile_at(t, offset=0):
        return pl.ds(pl.multiple_of(offset + t * tile, 16), tile)

    def inner(base, weight, t):
        both = jnp.concatenate([around(base, t), around(base + 1, t)], axis=1)
        acc[tile_at(t), :] = dot(both, weight[...])

    def face_tile(base, face, make, t):
        for side, has in ((0, has_left), (1, has_right)):
            arrive(make, side, t, has)
            stack_tile(base + 2 + side, face.at[side], t)

    def one_layer(layer, weight, t):
        at = pl.ds(pl.multiple_of(PAD + t * tile, 16), tile + PAD)
        both = jnp.concatenate([odd[layer, at, :], even[layer, at, :]], axis=1)
        total = dot(both, weight)
        return total[:tile, :channels] + total[depth : tile + depth, channels:]

    def outer(base, weight, side, t):
        return acc[tile_at(t), side * channels : (side + 1) * channels] + one_layer(
            base + 2 + side, weight[side], t
        )

    def repeat(count, body):
        def step(t, carry):
            body(t)
            return carry

        lax.fori_loop(0, count, step, 0)

    cells = tile // depth
    cube = (cells, depth, across)

    def spread_tile(t):
        lane = lax.broadcasted_iota(jnp.int32, cube, 2)
        cell = lax.broadcasted_iota(jnp.int32, cube, 0) + t * cells
        for side in range(2):
            field = jnp.broadcast_to(prior[side][None], cube)
            field = jnp.sum(jnp.where(lane == cell, field, 0.0), axis=2, keepdims=True)
            field = jnp.broadcast_to(field, (cells, depth, channels))
            spread[side, tile_at(t), :] = field.reshape(tile, channels)

    for copy in vox_loads + loads[:8]:
        copy.wait()

    @functools.partial(repeat, tiles + 1)
    def _(t):
        @pl.when(t < tiles)
        def _():
            for side in range(2):
                stack_tile(side, vox.at[side], t)

        @pl.when(t == tiles)
        def _():
            for side in range(2):
                stack_end(side, vox.at[side])

        @pl.when(t >= 1)
        def _():
            spread_tile(t - 1)
            inner(0, w_first, t - 1)

    for copy in loads[8:]:
        copy.wait()

    @functools.partial(repeat, tiles + 2)
    def _(t):
        @pl.when(t < tiles)
        def _():
            face_tile(0, face_vox, vox_copy, t)

        @pl.when(t == tiles)
        def _():
            for side in range(2):
                stack_end(2 + side, face_vox.at[side])

        @pl.when(jnp.logical_and(t >= 1, t <= tiles))
        def _():
            u = t - 1
            for side, has in ((0, has_left), (1, has_right)):
                value = activate(outer(0, w_face.at[0], side, u)).astype(BF16)
                first[side, tile_at(u, PAD), :] = value

                @pl.when(has)
                def _():
                    first_copy(side, u).start()

            for side in range(2):
                stack_tile(4 + side, first.at[side], u)

        @pl.when(t == tiles)
        def _():
            for side in range(2):
                stack_end(4 + side, first.at[side])

        @pl.when(t >= 2)
        def _():
            inner(4, w_second, t - 2)

    running[:, 0] = jnp.full((2, depth, channels), -jnp.inf, F32)
    running[:, 1:] = jnp.zeros((2, 2, depth, channels), F32)

    def local_part(t):
        logits, features = [], []
        for side in range(2):
            value = outer(4, w_face.at[1], side, t)
            value += vox[side, tile_at(t, PAD), :].astype(F32)
            value = value.astype(BF16)
            feature[side, tile_at(t), :] = value
            both = dot(value, w_score[...])
            field = spread[side, tile_at(t), :]
            value = value.astype(F32)
            logits.append(both[:, :channels] + field)
            features.append(value)
            logit_y = (both[:, channels:] + field).reshape(cells, depth, channels)
            value = value.reshape(cells, depth, channels)
            old, norm, total = running[side, 0], running[side, 1], running[side, 2]
            peak = jnp.maximum(jnp.max(logit_y, axis=0), old)
            weight = jnp.exp(logit_y - peak[None])
            keep = jnp.exp(old - peak)
            running[side, 0] = peak
            running[side, 1] = norm * keep + jnp.sum(weight, 0)
            running[side, 2] = total * keep + jnp.sum(weight * value, 0)
        peak = jnp.maximum(logits[0], logits[1]).astype(BF16)
        weights = [jnp.exp(logit - peak.astype(F32)) for logit in logits]
        stats[0, tile_at(t), :] = peak
        stats[1, tile_at(t), :] = (weights[0] + weights[1]).astype(BF16)
        stats[2, tile_at(t), :] = (weights[0] * features[0] + weights[1] * features[1]).astype(BF16)

    def rows_at(start, rows):
        return pl.ds(pl.multiple_of(start, 16), rows)

    def start_of(g, k):
        start = g * tile
        for digit, (_, _, rows, shares) in zip(digits[:k], stages):
            if shares:
                start = start + digit * rows
        return start

    def reduce_copies(g, k):
        distance, radix, rows, shares = stages[k]
        copies = []
        for hop in range(1, radix):
            partner, theirs = partners[k][hop]
            give = start_of(g, k)
            if shares:
                give = give + theirs * rows
            copies.append(
                pltpu.make_async_remote_copy(
                    src_ref=stats.at[:, rows_at(give, rows), :],
                    dst_ref=halves[k].at[g, hop - 1],
                    send_sem=rs_send.at[g, slots[k] + hop - 1],
                    recv_sem=rs_recv.at[g, slots[k] + hop - 1],
                    device_id={"gx": partner},
                    device_id_type=MESH,
                )
            )
        return copies

    def reduce_end(g, k):
        distance, radix, rows, shares = stages[k]
        for copy in reduce_copies(g, k):
            copy.wait_recv()
            if not shares:
                copy.wait_send()
        start = start_of(g, k + 1)
        at = rows_at(start, rows)
        held = [stats[:, at, :].astype(F32)]
        held += [halves[k][g, hop].astype(F32) for hop in range(radix - 1)]
        peak = functools.reduce(jnp.maximum, [each[0] for each in held])
        scales = [jnp.exp(each[0] - peak) for each in held]
        norm = sum(each[1] * scale for each, scale in zip(held, scales))
        total = sum(each[2] * scale for each, scale in zip(held, scales))
        if k + 1 < len(stages):
            for i, value in enumerate((peak, norm, total)):
                stats[i, at, :] = value.astype(BF16)
        else:
            pooled[rows_at(PAD + start, rows), :] = (total / norm).astype(BF16)

    def gather_copy(g, slot, start, rows, partner):
        part = pooled.at[rows_at(PAD + start, rows), :]
        return pltpu.make_async_remote_copy(
            src_ref=part,
            dst_ref=part,
            send_sem=ag_send.at[g, slot],
            recv_sem=ag_recv.at[g, slot],
            device_id={"gx": partner},
            device_id_type=MESH,
        )

    def far_copies(g):
        start, rows = start_of(g, len(stages)), stages[-1][2]
        return [gather_copy(g, i, start, rows, partner) for i, partner in enumerate(far)]

    def strip_copy(side):
        return pltpu.make_async_remote_copy(
            src_ref=strip.at[1 + side],
            dst_ref=strip.at[3 - 3 * side],
            send_sem=strip_send.at[side],
            recv_sem=strip_recv.at[1 - side],
            device_id={"gx": (left, right)[side]},
            device_id_type=MESH,
        )

    def strip_start():
        for side, has in ((0, has_left), (1, has_right)):
            strip[1 + side] = (running[side, 2] / running[side, 1]).astype(BF16).astype(F32)

            @pl.when(has)
            def _():
                strip_copy(side).start()

    def strip_plane():
        for side, has in ((0, has_left), (1, has_right)):

            @pl.when(has)
            def _():
                strip_copy(1 - side).wait_recv()

        moved = shifted(strip[...])
        stacked = [
            jnp.concatenate([part[x + i] for i in range(3) for part in moved], axis=1)
            for x in range(2)
        ]
        plane = dot(jnp.concatenate(stacked, axis=0).astype(BF16), w_xz[...])
        plane_xz[...] = plane.astype(BF16).astype(F32)

    def finish(t):
        plane_yz = one_layer(8, w_yz[...], t)
        plane_yz = plane_yz.astype(BF16).astype(F32).reshape(cells, depth, channels)
        for side in range(2):
            mixing = plane_yz + plane_xz[side * depth : (side + 1) * depth, :][None]
            joined = feature[side, tile_at(t), :].astype(F32) * mixing.reshape(tile, channels)
            squares = dot((joined * joined).astype(BF16), jnp.ones((channels, channels), BF16))
            scale = lax.rsqrt(squares * (1.0 / channels) + 1e-06)
            normed = (joined * scale * norm_gain[...]).astype(BF16)
            hidden = activate(dot(normed, w_in[...])).astype(BF16)
            out[side, tile_at(t), :] = (joined + dot(hidden, w_out[...])).astype(BF16)

    last = len(stages)

    @functools.partial(repeat, tiles + last + 3)
    def _(slot):
        @pl.when(slot < tiles)
        def _():
            face_tile(4, face_first, first_copy, slot)

        @pl.when(slot == tiles)
        def _():
            for side in range(2):
                stack_end(6 + side, face_first.at[side])

        @pl.when(jnp.logical_and(slot >= 1, slot <= tiles))
        def _():
            local_part(slot - 1)

        def at_step(step, body):
            g = slot - 1 - step

            @pl.when(jnp.logical_and(g >= 0, g < tiles))
            def _():
                body(g)

        def start_all(copies):
            for copy in copies:
                copy.start()

        def end_all(copies):
            for copy in copies:
                copy.wait_recv()

        def advance(k, g):
            if k > 0:
                reduce_end(g, k - 1)
            start_all(reduce_copies(g, k) if k < last else far_copies(g))

        def gather_end(g):
            end_all(far_copies(g))
            stack_tile(8, pooled, g)

            @pl.when(g == tiles - 1)
            def _():
                stack_end(8, pooled)

        for k in range(last + 1):
            at_step(k, functools.partial(advance, k))
        at_step(last + 1, gather_end)

        @pl.when(slot == tiles)
        def _():
            strip_start()

        @pl.when(slot == tiles + 1)
        def _():
            strip_plane()

        at_step(last + 2, finish)

    @functools.partial(repeat, tiles)
    def _(g):
        for k, (_, _, _, shares) in enumerate(stages):
            for copy in reduce_copies(g, k) if shares else []:
                copy.wait_send()
        for copy in far_copies(g):
            copy.wait_send()

    sent(vox_copy)
    sent(first_copy)
    for side, has in ((0, has_left), (1, has_right)):

        @pl.when(has)
        def _():
            strip_copy(side).wait_send()


def on_device(
    n,
    voxels,
    prior,
    conv_first,
    conv_second,
    score_x,
    score_y,
    plane_yz_w,
    plane_xz_w,
    norm_gain,
    mlp_in,
    mlp_out,
):
    rows, across, depth, channels = voxels.shape
    assert rows == 2 and depth == 8 and n & (n - 1) == 0
    length = across * depth
    hidden = mlp_in.shape[1]
    tile = min(512, length)
    tiles = length // tile
    stages = stages_of(tile, n)
    exchanges = sum(stage[1] - 1 for stage in stages)
    padded = length + 2 * PAD
    taps = conv_first.shape[0] // 3 * channels
    hbm = pl.BlockSpec(memory_space=pl.ANY)
    vmem = pl.BlockSpec(memory_space=pltpu.VMEM)
    result = pl.pallas_call(
        functools.partial(kernel, n, tile, stages),
        out_shape=jax.ShapeDtypeStruct((rows, length, channels), BF16),
        in_specs=[hbm, vmem, hbm, hbm, hbm, hbm, hbm, hbm, vmem, hbm, hbm],
        out_specs=vmem,
        scratch_shapes=[
            pltpu.VMEM((2 * taps, 2 * channels), BF16),
            pltpu.VMEM((2 * taps, 2 * channels), BF16),
            pltpu.VMEM((2, 2, 2 * taps // 3, 2 * channels), BF16),
            pltpu.VMEM((channels, 2 * channels), BF16),
            pltpu.VMEM((2 * taps // 3, 2 * channels), BF16),
            pltpu.VMEM((taps, channels), BF16),
            pltpu.VMEM((channels, hidden), BF16),
            pltpu.VMEM((hidden, channels), BF16),
            pltpu.VMEM((2, padded, channels), BF16),
            pltpu.VMEM((2, padded, channels), BF16),
            pltpu.VMEM((2, padded, channels), BF16),
            pltpu.VMEM((2, padded, channels), BF16),
            pltpu.VMEM((length, 2 * channels), F32),
            pltpu.VMEM((2, length, channels), BF16),
            pltpu.VMEM((3, length, channels), BF16),
            pltpu.VMEM((padded, channels), BF16),
            pltpu.VMEM((4, depth, channels), F32),
            pltpu.VMEM((2, 3, depth, channels), F32),
            pltpu.VMEM((2 * depth, channels), F32),
            pltpu.VMEM((2, length, channels), F32),
            pltpu.VMEM((9, padded, 3 * channels), BF16),
            pltpu.VMEM((9, padded, 3 * channels), BF16),
            [
                pltpu.VMEM((tiles, radix - 1, 3, share, channels), BF16)
                for _, radix, share, _ in stages
            ],
            pltpu.SemaphoreType.DMA((23,)),
            pltpu.SemaphoreType.DMA((2,)),
            pltpu.SemaphoreType.DMA((2, 2, tiles)),
            pltpu.SemaphoreType.DMA((2, 2, tiles)),
            pltpu.SemaphoreType.DMA((2,)),
            pltpu.SemaphoreType.DMA((2,)),
            pltpu.SemaphoreType.DMA((tiles, exchanges)),
            pltpu.SemaphoreType.DMA((tiles, exchanges)),
            pltpu.SemaphoreType.DMA((tiles, far_radix(stages))),
            pltpu.SemaphoreType.DMA((tiles, far_radix(stages))),
        ],
        compiler_params=pltpu.CompilerParams(
            collective_id=0, has_side_effects=True, vmem_limit_bytes=62 * 1024 * 1024
        ),
    )(
        voxels.reshape(rows, length, channels),
        prior.transpose(0, 2, 1),
        conv_first.reshape(3, taps, channels),
        conv_second.reshape(3, taps, channels),
        score_x,
        score_y,
        plane_yz_w.reshape(taps, channels),
        plane_xz_w.reshape(taps, channels),
        norm_gain.reshape(1, channels),
        mlp_in,
        mlp_out,
    )
    return result.reshape(voxels.shape)


def solution(mesh):
    split = P(("scene", "gx"), None, None, None)
    return jax.shard_map(
        functools.partial(on_device, mesh.shape["gx"]),
        mesh=mesh,
        in_specs=(split, P(("scene", "gx"), None, None)) + (P(),) * 9,
        out_specs=split,
        check_vma=False,
    )
```

```python
import functools

import jax
import jax.numpy as jnp
from jax import lax
from jax.experimental import pallas as pl
from jax.experimental.pallas import tpu as pltpu
from jax.sharding import PartitionSpec as P

MESH = pl.DeviceIdType.MESH
PAD = 16
F32 = jnp.float32
BF16 = jnp.bfloat16


def activate(values):
    return jax.nn.gelu(values, approximate=True)


def stages_of(rows, devices):
    count = devices.bit_length() - 1
    bits = [[i] for i in range(min(2, count))]
    bits += [list(range(i, min(i + 2, count))) for i in range(2, count, 2)]
    stages = []
    for group in bits:
        radix = 1 << len(group)
        shares = rows % (16 * radix) == 0
        rows = rows // radix if shares else rows
        stages.append((1 << group[0], radix, rows, shares))
    return stages


def far_radix(stages):
    total = 1
    for distance, radix, _, shares in stages:
        if shares and distance > 1:
            total *= radix
    return total


def shifted(values):
    depth = values.shape[1]
    at_z = lax.broadcasted_iota(jnp.int32, (1,) + values.shape[1:], 1)
    below = jnp.where(at_z == 0, 0.0, pltpu.roll(values, 1, 1))
    above = jnp.where(at_z == depth - 1, 0.0, pltpu.roll(values, depth - 1, 1))
    return below, values, above


def stack(source, even, odd, start, rows, depth):
    channels = source.shape[1]
    window = source[pl.ds(pl.multiple_of(start - PAD, 16), rows + PAD), :].astype(F32)
    parts = shifted(window.reshape(-1, depth, channels))
    at = pl.ds(pl.multiple_of(start, 16), rows)
    for i, part in enumerate(parts):
        part = part.reshape(rows + PAD, channels)
        columns = slice(i * channels, (i + 1) * channels)
        even[at, columns] = part[PAD:].astype(BF16)
        odd[at, columns] = part[PAD - depth : rows + PAD - depth].astype(BF16)


def neighbourhood(even, odd, start, tile):
    first = pl.ds(pl.multiple_of(start, 16), tile)
    after = pl.ds(pl.multiple_of(start + PAD, 16), tile)
    return jnp.concatenate([odd[first, :], even[first, :], odd[after, :]], axis=1)


def dot(a, b):
    return jnp.dot(a, b, preferred_element_type=F32)


def kernel(
    n,
    tile,
    stages,
    voxels,
    prior,
    conv_first,
    conv_second,
    score_x,
    score_y,
    plane_yz_w,
    plane_xz_w,
    norm_gain,
    mlp_in,
    mlp_out,
    out,
    w_first,
    w_second,
    w_score,
    w_yz,
    w_xz,
    w_in,
    w_out,
    vox,
    face_vox,
    first,
    face_first,
    acc,
    feature,
    stats,
    pooled,
    strip,
    running,
    plane_xz,
    spread,
    even,
    odd,
    halves,
    load_sem,
    vox_sem,
    face_send,
    face_recv,
    strip_send,
    strip_recv,
    rs_send,
    rs_recv,
    ag_send,
    ag_recv,
):
    me = lax.axis_index("gx")
    length, channels = voxels.shape[1], voxels.shape[2]
    depth = prior.shape[1]
    tiles = length // tile
    has_left, has_right = me > 0, me < n - 1
    left, right = me - 1, me + 1
    across = length // depth

    def across_bits(distance, hop):
        other, weight = me, 1
        while weight <= hop:
            bit = (me // (distance * weight)) % 2
            if hop & weight:
                other = other + (1 - 2 * bit) * distance * weight
            weight *= 2
        return other

    digits = [(me // distance) % radix for distance, radix, _, _ in stages]
    partners = []
    for distance, radix, _, _ in stages:
        found = {}
        for hop in range(1, radix):
            other = across_bits(distance, hop)
            found[hop] = (other, (other // distance) % radix)
        partners.append(found)
    slots = [sum(stage[1] - 1 for stage in stages[:k]) for k in range(len(stages))]
    far = [across_bits(2, hop) for hop in range(1, far_radix(stages))]

    taps = conv_first.shape[1]
    loads = []
    for source, target in ((conv_first, w_first), (conv_second, w_second)):
        for layer in range(2):
            for result in range(2):
                block = (pl.ds(layer * taps, taps), pl.ds(result * channels, channels))
                loads.append((source.at[1 + layer - result], target.at[block]))
    loads += [
        (score_x, w_score.at[:, pl.ds(0, channels)]),
        (score_y, w_score.at[:, pl.ds(channels, channels)]),
        (plane_yz_w, w_yz),
        (plane_xz_w, w_xz),
        (mlp_in, w_in),
        (mlp_out, w_out),
    ]
    vox_loads = [
        pltpu.make_async_copy(
            voxels.at[row], vox.at[row, pl.ds(PAD, length), :], vox_sem.at[row]
        )
        for row in range(2)
    ]
    loads = [
        pltpu.make_async_copy(source, target, load_sem.at[i])
        for i, (source, target) in enumerate(loads)
    ]
    barrier = pltpu.get_barrier_semaphore()
    greeted = far + [
        partner
        for stage, found in zip(stages, partners)
        for partner, _ in found.values()
        if stage[0] == 1 or not stage[3]
    ]
    for partner in greeted:
        pl.semaphore_signal(barrier, inc=1, device_id={"gx": partner}, device_id_type=MESH)

    @pl.when(has_left)
    def _():
        pl.semaphore_signal(barrier, inc=1, device_id={"gx": left}, device_id_type=MESH)

    @pl.when(has_right)
    def _():
        pl.semaphore_signal(barrier, inc=1, device_id={"gx": right}, device_id_type=MESH)

    for copy in vox_loads:
        copy.start()

    edge = jnp.zeros((2, PAD, channels), BF16)
    for padded in (vox, face_vox, first, face_first):
        padded[:, 0:PAD, :] = edge
        padded[:, PAD + length :, :] = edge
    pooled[0:PAD, :] = edge[0]
    pooled[PAD + length :, :] = edge[0]

    for side, has in ((0, has_left), (1, has_right)):

        @pl.when(jnp.logical_not(has))
        def _():
            blank = jnp.zeros((length, channels), BF16)
            face_vox[side, pl.ds(PAD, length), :] = blank
            face_first[side, pl.ds(PAD, length), :] = blank
            strip[3 * side] = jnp.zeros(strip.shape[1:], F32)

    pl.semaphore_wait(barrier, len(greeted) + jnp.where(has_left, 1, 0) + jnp.where(has_right, 1, 0))

    def face_copy(which, source, target, side, t, to):
        return pltpu.make_async_remote_copy(
            src_ref=source,
            dst_ref=target.at[1 - side, pl.ds(pl.multiple_of(PAD + t * tile, 16), tile), :],
            send_sem=face_send.at[which, side, t],
            recv_sem=face_recv.at[which, 1 - side, t],
            device_id={"gx": to},
            device_id_type=MESH,
        )

    def vox_copy(side, t):
        source = voxels.at[side, pl.ds(pl.multiple_of(t * tile, 16), tile), :]
        return face_copy(0, source, face_vox, side, t, (left, right)[side])

    def first_copy(side, t):
        source = first.at[side, pl.ds(pl.multiple_of(PAD + t * tile, 16), tile), :]
        return face_copy(1, source, face_first, side, t, (left, right)[side])

    def arrive(make, side, t, has):
        @pl.when(has)
        def _():
            make(1 - side, t).wait_recv()

    def sent(make):
        for side, has in ((0, has_left), (1, has_right)):

            @pl.when(has)
            def _():
                for t in range(tiles):
                    make(side, t).wait_send()

    for t in range(tiles):
        for side, has in ((0, has_left), (1, has_right)):

            @pl.when(has)
            def _():
                vox_copy(side, t).start()

    for copy in loads:
        copy.start()

    def stack_tile(layer, source, t):
        stack(source, even.at[layer], odd.at[layer], PAD + t * tile, tile, depth)

    def stack_end(layer, source):
        stack(source, even.at[layer], odd.at[layer], PAD + length, PAD, depth)

    def around(layer, t):
        return neighbourhood(even.at[layer], odd.at[layer], PAD + t * tile, tile)

    def tile_at(t, offset=0):
        return pl.ds(pl.multiple_of(offset + t * tile, 16), tile)

    def inner(base, weight, t):
        both = jnp.concatenate([around(base, t), around(base + 1, t)], axis=1)
        acc[tile_at(t), :] = dot(both, weight[...])

    def face_tile(base, face, make, t):
        for side, has in ((0, has_left), (1, has_right)):
            arrive(make, side, t, has)
            stack_tile(base + 2 + side, face.at[side], t)

    def outer(base, weight, side, t):
        if side == 0:
            part = weight[:taps, channels:]
        else:
            part = weight[taps:, :channels]
        return acc[tile_at(t), side * channels : (side + 1) * channels] + dot(
            around(base + 2 + side, t), part
        )

    def repeat(count, body):
        def step(t, carry):
            body(t)
            return carry

        lax.fori_loop(0, count, step, 0)

    cells = tile // depth
    cube = (cells, depth, across)

    def spread_tile(t):
        lane = lax.broadcasted_iota(jnp.int32, cube, 2)
        cell = lax.broadcasted_iota(jnp.int32, cube, 0) + t * cells
        for side in range(2):
            field = jnp.broadcast_to(prior[side][None], cube)
            field = jnp.sum(jnp.where(lane == cell, field, 0.0), axis=2, keepdims=True)
            field = jnp.broadcast_to(field, (cells, depth, channels))
            spread[side, tile_at(t), :] = field.reshape(tile, channels)

    for copy in vox_loads + loads[:4]:
        copy.wait()

    @functools.partial(repeat, tiles + 1)
    def _(t):
        @pl.when(t < tiles)
        def _():
            for side in range(2):
                stack_tile(side, vox.at[side], t)

        @pl.when(t == tiles)
        def _():
            for side in range(2):
                stack_end(side, vox.at[side])

        @pl.when(t >= 1)
        def _():
            spread_tile(t - 1)
            inner(0, w_first, t - 1)

    for copy in loads[4:]:
        copy.wait()

    @functools.partial(repeat, tiles + 2)
    def _(t):
        @pl.when(t < tiles)
        def _():
            face_tile(0, face_vox, vox_copy, t)

        @pl.when(t == tiles)
        def _():
            for side in range(2):
                stack_end(2 + side, face_vox.at[side])

        @pl.when(jnp.logical_and(t >= 1, t <= tiles))
        def _():
            u = t - 1
            for side, has in ((0, has_left), (1, has_right)):
                value = activate(outer(0, w_first, side, u)).astype(BF16)
                first[side, tile_at(u, PAD), :] = value

                @pl.when(has)
                def _():
                    first_copy(side, u).start()

            for side in range(2):
                stack_tile(4 + side, first.at[side], u)

        @pl.when(t == tiles)
        def _():
            for side in range(2):
                stack_end(4 + side, first.at[side])

        @pl.when(t >= 2)
        def _():
            inner(4, w_second, t - 2)

    running[:, 0] = jnp.full((2, depth, channels), -jnp.inf, F32)
    running[:, 1:] = jnp.zeros((2, 2, depth, channels), F32)

    def local_part(t):
        logits, features = [], []
        for side in range(2):
            value = outer(4, w_second, side, t)
            value += vox[side, tile_at(t, PAD), :].astype(F32)
            value = value.astype(BF16)
            feature[side, tile_at(t), :] = value
            both = dot(value, w_score[...])
            field = spread[side, tile_at(t), :]
            value = value.astype(F32)
            logits.append(both[:, :channels] + field)
            features.append(value)
            logit_y = (both[:, channels:] + field).reshape(cells, depth, channels)
            value = value.reshape(cells, depth, channels)
            old, norm, total = running[side, 0], running[side, 1], running[side, 2]
            peak = jnp.maximum(jnp.max(logit_y, axis=0), old)
            weight = jnp.exp(logit_y - peak[None])
            keep = jnp.exp(old - peak)
            running[side, 0] = peak
            running[side, 1] = norm * keep + jnp.sum(weight, 0)
            running[side, 2] = total * keep + jnp.sum(weight * value, 0)
        peak = jnp.maximum(logits[0], logits[1]).astype(BF16)
        weights = [jnp.exp(logit - peak.astype(F32)) for logit in logits]
        stats[0, tile_at(t), :] = peak
        stats[1, tile_at(t), :] = (weights[0] + weights[1]).astype(BF16)
        stats[2, tile_at(t), :] = (weights[0] * features[0] + weights[1] * features[1]).astype(BF16)

    def rows_at(start, rows):
        return pl.ds(pl.multiple_of(start, 16), rows)

    def start_of(g, k):
        start = g * tile
        for digit, (_, _, rows, shares) in zip(digits[:k], stages):
            if shares:
                start = start + digit * rows
        return start

    def reduce_copies(g, k):
        distance, radix, rows, shares = stages[k]
        copies = []
        for hop in range(1, radix):
            partner, theirs = partners[k][hop]
            give = start_of(g, k)
            if shares:
                give = give + theirs * rows
            copies.append(
                pltpu.make_async_remote_copy(
                    src_ref=stats.at[:, rows_at(give, rows), :],
                    dst_ref=halves[k].at[g, hop - 1],
                    send_sem=rs_send.at[g, slots[k] + hop - 1],
                    recv_sem=rs_recv.at[g, slots[k] + hop - 1],
                    device_id={"gx": partner},
                    device_id_type=MESH,
                )
            )
        return copies

    def reduce_end(g, k):
        distance, radix, rows, shares = stages[k]
        for copy in reduce_copies(g, k):
            copy.wait_recv()
            if not shares:
                copy.wait_send()
        start = start_of(g, k + 1)
        at = rows_at(start, rows)
        held = [stats[:, at, :].astype(F32)]
        held += [halves[k][g, hop].astype(F32) for hop in range(radix - 1)]
        peak = functools.reduce(jnp.maximum, [each[0] for each in held])
        scales = [jnp.exp(each[0] - peak) for each in held]
        norm = sum(each[1] * scale for each, scale in zip(held, scales))
        total = sum(each[2] * scale for each, scale in zip(held, scales))
        if k + 1 < len(stages):
            for i, value in enumerate((peak, norm, total)):
                stats[i, at, :] = value.astype(BF16)
        else:
            pooled[rows_at(PAD + start, rows), :] = (total / norm).astype(BF16)

    def gather_copy(g, slot, start, rows, partner):
        part = pooled.at[rows_at(PAD + start, rows), :]
        return pltpu.make_async_remote_copy(
            src_ref=part,
            dst_ref=part,
            send_sem=ag_send.at[g, slot],
            recv_sem=ag_recv.at[g, slot],
            device_id={"gx": partner},
            device_id_type=MESH,
        )

    def far_copies(g):
        start, rows = start_of(g, len(stages)), stages[-1][2]
        return [gather_copy(g, i, start, rows, partner) for i, partner in enumerate(far)]

    def near_copies(g):
        rows = stages[0][2]
        return [gather_copy(g, len(far), start_of(g, 1), rows, partners[0][1][0])]

    def strip_copy(side):
        return pltpu.make_async_remote_copy(
            src_ref=strip.at[1 + side],
            dst_ref=strip.at[3 - 3 * side],
            send_sem=strip_send.at[side],
            recv_sem=strip_recv.at[1 - side],
            device_id={"gx": (left, right)[side]},
            device_id_type=MESH,
        )

    def strip_start():
        for side, has in ((0, has_left), (1, has_right)):
            strip[1 + side] = (running[side, 2] / running[side, 1]).astype(BF16).astype(F32)

            @pl.when(has)
            def _():
                strip_copy(side).start()

    def strip_plane():
        for side, has in ((0, has_left), (1, has_right)):

            @pl.when(has)
            def _():
                strip_copy(1 - side).wait_recv()

        moved = shifted(strip[...])
        stacked = [
            jnp.concatenate([part[x + i] for i in range(3) for part in moved], axis=1)
            for x in range(2)
        ]
        plane = dot(jnp.concatenate(stacked, axis=0).astype(BF16), w_xz[...])
        plane_xz[...] = plane.astype(BF16).astype(F32)

    def finish(t):
        plane_yz = dot(around(8, t), w_yz[...])
        plane_yz = plane_yz.astype(BF16).astype(F32).reshape(cells, depth, channels)
        for side in range(2):
            mixing = plane_yz + plane_xz[side * depth : (side + 1) * depth, :][None]
            joined = feature[side, tile_at(t), :].astype(F32) * mixing.reshape(tile, channels)
            squares = dot((joined * joined).astype(BF16), jnp.ones((channels, channels), BF16))
            scale = lax.rsqrt(squares * (1.0 / channels) + 1e-06)
            normed = (joined * scale * norm_gain[...]).astype(BF16)
            hidden = activate(dot(normed, w_in[...])).astype(BF16)
            out[side, tile_at(t), :] = (joined + dot(hidden, w_out[...])).astype(BF16)

    last = len(stages)

    @functools.partial(repeat, tiles + last + 4)
    def _(slot):
        @pl.when(slot < tiles)
        def _():
            face_tile(4, face_first, first_copy, slot)

        @pl.when(slot == tiles)
        def _():
            for side in range(2):
                stack_end(6 + side, face_first.at[side])

        @pl.when(jnp.logical_and(slot >= 1, slot <= tiles))
        def _():
            local_part(slot - 1)

        def at_step(step, body):
            g = slot - 1 - step

            @pl.when(jnp.logical_and(g >= 0, g < tiles))
            def _():
                body(g)

        def start_all(copies):
            for copy in copies:
                copy.start()

        def end_all(copies):
            for copy in copies:
                copy.wait_recv()

        def advance(k, g):
            if k > 0:
                reduce_end(g, k - 1)
            start_all(reduce_copies(g, k) if k < last else far_copies(g))

        def gather_near(g):
            end_all(far_copies(g))
            start_all(near_copies(g))

        def gather_end(g):
            end_all(near_copies(g))
            stack_tile(8, pooled, g)

            @pl.when(g == tiles - 1)
            def _():
                stack_end(8, pooled)

        for k in range(last + 1):
            at_step(k, functools.partial(advance, k))
        at_step(last + 1, gather_near)
        at_step(last + 2, gather_end)

        @pl.when(slot == tiles)
        def _():
            strip_start()

        @pl.when(slot == tiles + 1)
        def _():
            strip_plane()

        at_step(last + 3, finish)

    @functools.partial(repeat, tiles)
    def _(g):
        for k, (_, _, _, shares) in enumerate(stages):
            for copy in reduce_copies(g, k) if shares else []:
                copy.wait_send()
        for copy in far_copies(g) + near_copies(g):
            copy.wait_send()

    sent(vox_copy)
    sent(first_copy)
    for side, has in ((0, has_left), (1, has_right)):

        @pl.when(has)
        def _():
            strip_copy(side).wait_send()


def on_device(
    n,
    voxels,
    prior,
    conv_first,
    conv_second,
    score_x,
    score_y,
    plane_yz_w,
    plane_xz_w,
    norm_gain,
    mlp_in,
    mlp_out,
):
    rows, across, depth, channels = voxels.shape
    assert rows == 2 and depth == 8 and n & (n - 1) == 0
    length = across * depth
    hidden = mlp_in.shape[1]
    tile = min(512, length)
    tiles = length // tile
    stages = stages_of(tile, n)
    exchanges = sum(stage[1] - 1 for stage in stages)
    padded = length + 2 * PAD
    taps = conv_first.shape[0] // 3 * channels
    hbm = pl.BlockSpec(memory_space=pl.ANY)
    vmem = pl.BlockSpec(memory_space=pltpu.VMEM)
    result = pl.pallas_call(
        functools.partial(kernel, n, tile, stages),
        out_shape=jax.ShapeDtypeStruct((rows, length, channels), BF16),
        in_specs=[hbm, vmem, hbm, hbm, hbm, hbm, hbm, hbm, vmem, hbm, hbm],
        out_specs=vmem,
        scratch_shapes=[
            pltpu.VMEM((2 * taps, 2 * channels), BF16),
            pltpu.VMEM((2 * taps, 2 * channels), BF16),
            pltpu.VMEM((channels, 2 * channels), BF16),
            pltpu.VMEM((taps, channels), BF16),
            pltpu.VMEM((taps, channels), BF16),
            pltpu.VMEM((channels, hidden), BF16),
            pltpu.VMEM((hidden, channels), BF16),
            pltpu.VMEM((2, padded, channels), BF16),
            pltpu.VMEM((2, padded, channels), BF16),
            pltpu.VMEM((2, padded, channels), BF16),
            pltpu.VMEM((2, padded, channels), BF16),
            pltpu.VMEM((length, 2 * channels), F32),
            pltpu.VMEM((2, length, channels), BF16),
            pltpu.VMEM((3, length, channels), BF16),
            pltpu.VMEM((padded, channels), BF16),
            pltpu.VMEM((4, depth, channels), F32),
            pltpu.VMEM((2, 3, depth, channels), F32),
            pltpu.VMEM((2 * depth, channels), F32),
            pltpu.VMEM((2, length, channels), F32),
            pltpu.VMEM((9, padded, 3 * channels), BF16),
            pltpu.VMEM((9, padded, 3 * channels), BF16),
            [
                pltpu.VMEM((tiles, radix - 1, 3, share, channels), BF16)
                for _, radix, share, _ in stages
            ],
            pltpu.SemaphoreType.DMA((14,)),
            pltpu.SemaphoreType.DMA((2,)),
            pltpu.SemaphoreType.DMA((2, 2, tiles)),
            pltpu.SemaphoreType.DMA((2, 2, tiles)),
            pltpu.SemaphoreType.DMA((2,)),
            pltpu.SemaphoreType.DMA((2,)),
            pltpu.SemaphoreType.DMA((tiles, exchanges)),
            pltpu.SemaphoreType.DMA((tiles, exchanges)),
            pltpu.SemaphoreType.DMA((tiles, far_radix(stages))),
            pltpu.SemaphoreType.DMA((tiles, far_radix(stages))),
        ],
        compiler_params=pltpu.CompilerParams(
            collective_id=0, has_side_effects=True, vmem_limit_bytes=62 * 1024 * 1024
        ),
    )(
        voxels.reshape(rows, length, channels),
        prior.transpose(0, 2, 1),
        conv_first.reshape(3, taps, channels),
        conv_second.reshape(3, taps, channels),
        score_x,
        score_y,
        plane_yz_w.reshape(taps, channels),
        plane_xz_w.reshape(taps, channels),
        norm_gain.reshape(1, channels),
        mlp_in,
        mlp_out,
    )
    return result.reshape(voxels.shape)


def solution(mesh):
    split = P(("scene", "gx"), None, None, None)
    return jax.shard_map(
        functools.partial(on_device, mesh.shape["gx"]),
        mesh=mesh,
        in_specs=(split, P(("scene", "gx"), None, None)) + (P(),) * 9,
        out_specs=split,
        check_vma=False,
    )
```
